512 devices in a mesh: tgt: 32 (over z, x), src: 16 (over y, core).
Axes of the slice: x: 4, y: 8, z: 8, core: 2. Of those that a mesh axis runs over, the one named last changes fastest.
Arguments:
- src_emb: bfloat16 [16384, 300], P('src'), may hold values from -4 to 4
- tgt_emb: bfloat16 [131072, 300], P('tgt'), may hold values from -5 to 5
- g_init: float32 [131072], P('tgt'), may hold values from -1 to 1
- log_src: float32 [16384], P('src'), may hold values from -2 to 2
- log_tgt: float32 [131072], P('tgt'), may hold values from -2 to 2
- cand_ids: int32 [32, 128], P('src'), may hold values from 0 to 255, as said below
- cand_count: int32 [32], P('src'), may hold values from 8 to 128, as said below
Outputs:
- row_potential: float32 [16384], P('src')
- col_potential: float32 [131072], P('tgt')
- mapped: bfloat16 [16384, 300], P('src')
- row_mass: float32 [16384], P('src')
The draws below stay inside these ranges and needn't reach their ends.
Inputs may be any that keep to these rules, and one draw needn't show every extreme that they name: `cand_ids`: target block ids; every target block is a live candidate of some source block; slots at or past the count are ignored. `cand_count`: live slots of a source block.
All inputs are finite; a program needn't handle non-finite values.
Results may differ from the reference program's by a relative error of at most 0.0045.
Values may be sent and summed in bfloat16 or wider, within the bound.
No kernel may reach another device: no remote copies, remote signals or barrier semaphores. Data moves between devices by JAX's collectives and lax.ppermute only.
A program may use at most 128 MiB of HBM per device.

```python
import math
import jax
import jax.numpy as jnp
from jax import lax

E = 300
BLOCK = 512
NS = 16384
NT = 131072
NSB = 32
NTB = 256
R = 8
K = 128


def pattern(key):
    perm = jax.random.permutation(jax.random.fold_in(key, 101), NTB).astype(jnp.int32)
    forced = perm.reshape(NSB, R)
    extra = jax.random.randint(jax.random.fold_in(key, 102), (NSB, K - R), 0, NTB).astype(jnp.int32)
    ids = jnp.concatenate([forced, extra], axis=1)
    counts = jax.random.randint(jax.random.fold_in(key, 103), (NSB,), R, K + 1).astype(jnp.int32)
    fullest = jax.random.randint(jax.random.fold_in(key, 104), (), 0, NSB)
    offset = jax.random.randint(jax.random.fold_in(key, 105), (), 0, NSB - 1)
    emptiest = (fullest + 1 + offset) % NSB
    counts = counts.at[fullest].set(K).at[emptiest].set(R)
    return (ids, counts)


def field(key):
    return jnp.clip(jax.random.normal(jax.random.fold_in(key, 201), (NT, E), jnp.float32), -5.0, 5.0)


def draw_tgt_emb(key, part):
    base = field(key)
    return base.astype(jnp.bfloat16)


def draw_cand_ids(key, part):
    ids, counts = pattern(key)
    return ids


def draw_cand_count(key, part):
    ids, counts = pattern(key)
    return counts


def draw_src_emb(key, part):
    key = jax.random.fold_in(key, 4)
    scales = 0.4 * jnp.exp(jax.random.uniform(jax.random.fold_in(key, 1), (NS, 1), jnp.float32, 0.0, math.log(8.0)))
    raw = jnp.clip(jax.random.normal(jax.random.fold_in(key, 3), (NS, E), jnp.float32), -5.0, 5.0)
    values = raw * scales / math.sqrt(E)
    return jnp.clip(values, -4.0, 4.0).astype(jnp.bfloat16)


def level_of(rng, dims, split, low, high):
    factor_of, own = 1.0, jax.random.fold_in(rng, 6)
    for dim, parts in split:
        draws = jnp.exp(jax.random.uniform(jax.random.fold_in(own, dim), (parts,), jnp.float32, low / len(split), high / len(split)))
        factor_of = factor_of * jnp.repeat(draws, dims[dim] // parts).reshape([-1 if axis == dim else 1 for axis in range(len(dims))])
    return factor_of


def scatter_about(stream_key, extent, scale, reach, split=(), kind=jnp.bfloat16):
    gain = level_of(stream_key, extent, split, -0.22, 0.18) if split else 1.0
    result = jax.random.normal(stream_key, extent, jnp.float32) * scale * gain
    return jnp.minimum(jnp.maximum(result, -reach), reach).astype(kind)


def setup_inputs(seed: int = 0) -> dict:
    keys = jax.random.split(jax.random.key(seed), 8)
    return {
        "src_emb": draw_src_emb(jax.random.fold_in(keys[7], 71), 0),
        "tgt_emb": draw_tgt_emb(jax.random.fold_in(keys[7], 71), 0),
        "g_init": scatter_about(keys[2], (NT,), 0.2, 1.0, ((0, 32),), jnp.float32),
        "log_src": jnp.clip(jax.random.uniform(keys[3], (NS,), jnp.float32, -2.0, 2.0) * level_of(keys[3], (NS,), ((0, 16),), -0.4, 0.0), -2.0, 2.0),
        "log_tgt": jnp.clip(jax.random.uniform(keys[4], (NT,), jnp.float32, -2.0, 2.0) * level_of(keys[4], (NT,), ((0, 32),), -0.4, 0.0), -2.0, 2.0),
        "cand_ids": draw_cand_ids(jax.random.fold_in(keys[7], 71), 0),
        "cand_count": draw_cand_count(jax.random.fold_in(keys[7], 71), 0),
    }


EPS = 0.2
NEG = -1.0e30


def reference(src_emb, tgt_emb, g_init, log_src, log_tgt, cand_ids, cand_count):
    width = src_emb.shape[1]
    src_blocks = cand_ids.shape[0]
    slots = cand_ids.shape[1]
    tgt_blocks = tgt_emb.shape[0] // BLOCK
    xb = src_emb.reshape(src_blocks, BLOCK, width)
    yb = tgt_emb.reshape(tgt_blocks, BLOCK, width)
    order = jnp.arange(slots, dtype=jnp.int32)
    live = order[None, :] < cand_count[:, None]
    same = cand_ids[:, :, None] == cand_ids[:, None, :]
    earlier = order[None, :] < order[:, None]
    repeat = jnp.any(same & earlier[None] & live[:, None, :], axis=2)
    valid = live & jnp.logical_not(repeat)
    g_blocks = g_init.reshape(tgt_blocks, BLOCK)

    def block_scores(index):
        rows = xb[index].astype(jnp.float32)
        ids = cand_ids[index]
        cols = yb[ids].astype(jnp.float32)
        scores = jnp.einsum('ie,kje->ikj', rows, cols)
        return scores, cols, ids, valid[index][None, :, None]

    def row_pass(index):
        scores, cols, ids, okb = block_scores(index)
        z = jnp.where(okb, (g_blocks[ids][None] + scores) / EPS, NEG)
        peak = jnp.max(z, axis=(1, 2))
        total = jnp.sum(jnp.where(okb, jnp.exp(z - peak[:, None, None]), 0.0), axis=(1, 2))
        return peak + jnp.log(total)

    blocks_all = jnp.arange(src_blocks, dtype=jnp.int32)
    lse = lax.map(row_pass, blocks_all).reshape(-1)
    row_potential = EPS * log_src - EPS * lse
    f_blocks = row_potential.reshape(src_blocks, BLOCK)

    def col_pass(carry, index):
        cpeak, ctotal = carry
        scores, cols, ids, okb = block_scores(index)
        y = jnp.where(okb, (f_blocks[index][:, None, None] + scores) / EPS, NEG)
        tpeak = jnp.max(y, axis=0)
        ttotal = jnp.sum(jnp.where(okb, jnp.exp(y - tpeak[None]), 0.0), axis=0)
        newpeak = cpeak.at[ids].max(tpeak)
        ctotal = ctotal * jnp.exp(cpeak - newpeak)
        ctotal = ctotal.at[ids].add(ttotal * jnp.exp(tpeak - newpeak[ids]))
        return (newpeak, ctotal), None

    start = (jnp.full((tgt_blocks, BLOCK), NEG, jnp.float32), jnp.zeros((tgt_blocks, BLOCK), jnp.float32))
    (cpeak, ctotal), unused = lax.scan(col_pass, start, blocks_all)
    col_potential = EPS * log_tgt - EPS * (cpeak + jnp.log(ctotal)).reshape(-1)
    c_blocks = col_potential.reshape(tgt_blocks, BLOCK)

    def map_pass(index):
        scores, cols, ids, okb = block_scores(index)
        q = jnp.where(okb, (c_blocks[ids][None] + scores) / EPS, NEG)
        top = jnp.max(q, axis=(1, 2))
        weights = jnp.where(okb, jnp.exp(q - top[:, None, None]), 0.0).astype(jnp.bfloat16)
        weights = lax.optimization_barrier(weights).astype(jnp.float32)
        numer = jnp.einsum('ikj,kje->ie', weights, cols)
        denom = jnp.sum(weights, axis=(1, 2))
        return (numer / denom[:, None]).astype(jnp.bfloat16), top + jnp.log(denom)

    mapped, extra = lax.map(map_pass, blocks_all)
    mapped = mapped.reshape(-1, width)
    row_mass = row_potential / EPS + extra.reshape(-1)
    return row_potential, col_potential, mapped, row_mass
```

```python
import functools

import jax
import jax.numpy as jnp
from jax import lax
from jax.experimental import pallas as pl
from jax.experimental.pallas import tpu as pltpu
from jax.sharding import PartitionSpec as P

BLOCK = 512
LANES = 128
EPS = 0.2
INV = 5.0
NEG = -1e30
GROUPS = 4
CHUNK = 80
NT = (((1,), (1,)), ((), ()))
F32 = jnp.float32
BF16 = jnp.bfloat16


def logsum(values, axis):
    peak = jnp.max(values, axis=axis, keepdims=True)
    return peak + jnp.log(jnp.sum(jnp.exp(values - peak), axis=axis, keepdims=True))


def safe_log(peak, total):
    return jnp.where(total > 0.0, peak + jnp.log(jnp.where(total > 0.0, total, 1.0)), NEG)


def lane_parts(tile):
    return [tile[:, k * LANES : (k + 1) * LANES] for k in range(tile.shape[1] // LANES)]


def three_parts(value):
    high = value.astype(BF16).astype(F32)
    rest = value - high
    middle = rest.astype(BF16).astype(F32)
    return high, middle, rest - middle


def tiles(live_ref, body):
    blocks, columns = live_ref.shape

    def step(i, carry):
        b, t = i // columns, i % columns

        @pl.when(live_ref[b, t] > 0)
        def _():
            body(b, t)

        return carry

    lax.fori_loop(0, blocks * columns, step, 0)


def score(rows_ref, tgt_ref, b, t):
    rows = rows_ref[pl.ds(pl.multiple_of(b * BLOCK, BLOCK), BLOCK), :]
    cols = tgt_ref[:, pl.ds(pl.multiple_of(t * BLOCK, BLOCK), BLOCK)]
    return jnp.dot(rows[:, : cols.shape[0]], cols, preferred_element_type=F32)


def row_kernel(live_ref, src_ref, tgt_ref, g_ref, rows_ref, out_ref, pad, peak, total, packed):
    width, s_rows = src_ref.shape
    pad[...] = jnp.zeros_like(pad)
    pad[:width, :] = src_ref[...].astype(F32)
    for k in range(s_rows // LANES):
        piece = pad[:, k * LANES : (k + 1) * LANES]
        rows_ref[k * LANES : (k + 1) * LANES, :] = piece.T.astype(BF16)
    peak[...] = jnp.full_like(peak, NEG)
    total[...] = jnp.zeros_like(total)

    def body(b, t):
        g = g_ref[:, pl.ds(pl.multiple_of(t * BLOCK, BLOCK), BLOCK)] * INV
        z = lane_parts(score(rows_ref, tgt_ref, b, t) * INV + g)
        old = peak[b]
        new = functools.reduce(jnp.maximum, z, old)
        peak[b] = new
        total[b] = total[b] * jnp.exp(old - new) + sum(jnp.exp(part - new) for part in z)

    tiles(live_ref, body)
    per_block = BLOCK // LANES
    for b in range(s_rows // BLOCK):
        turned = peak[b].T
        top = jnp.max(turned, axis=0, keepdims=True)
        mass = jnp.sum(total[b].T * jnp.exp(turned - top), axis=0, keepdims=True)
        for k, part in enumerate(lane_parts(safe_log(top, mass))):
            packed[b * per_block + k : b * per_block + k + 1, :] = part
    out_ref[...] = jnp.broadcast_to(packed[...][None], out_ref.shape)


def col_kernel(live_ref, rows_ref, tgt_ref, lse_ref, log_ref, f_ref, out_ref, fcol, peak, total, packed):
    f = EPS * log_ref[...] - EPS * logsum(lse_ref[...], 0)[0]
    f_ref[...] = f
    for k in range(f.shape[0]):
        row = jnp.broadcast_to(f[k : k + 1, :] * INV, (LANES, LANES))
        fcol[k * LANES : (k + 1) * LANES, :] = row.T
    peak[...] = jnp.full_like(peak, NEG)
    total[...] = jnp.zeros_like(total)

    def body(b, t):
        own = fcol[pl.ds(pl.multiple_of(b * BLOCK, BLOCK), BLOCK), :]
        y = score(rows_ref, tgt_ref, b, t) * INV + jnp.concatenate([own] * (BLOCK // LANES), axis=1)
        y = y.reshape(BLOCK // 8, 8, BLOCK)
        old = peak[t]
        new = jnp.maximum(old, jnp.max(y, axis=0))
        peak[t] = new
        total[t] = total[t] * jnp.exp(old - new) + jnp.sum(jnp.exp(y - new[None]), axis=0)

    tiles(live_ref, body)
    per_block = BLOCK // LANES
    for t in range(peak.shape[0]):
        top = jnp.max(peak[t], axis=0, keepdims=True)
        mass = jnp.sum(total[t] * jnp.exp(peak[t] - top), axis=0, keepdims=True)
        for k, part in enumerate(lane_parts(safe_log(top, mass))):
            packed[t * per_block + k : t * per_block + k + 1, :] = part
    out_ref[...] = jnp.broadcast_to(packed[...][None], out_ref.shape)


def map_kernel(live_ref, rows_ref, tgt_ref, lse_ref, log_ref, c_ref, out_ref, crow, q, peak, denom, numer, buf):
    width = tgt_ref.shape[0]
    c = EPS * log_ref[...] - EPS * logsum(lse_ref[...], 0)[0]
    c_ref[...] = c
    for k in range(c.shape[0]):
        crow[:, k * LANES : (k + 1) * LANES] = c[k : k + 1, :] * INV
    blocks, columns = live_ref.shape
    peak[...] = jnp.full_like(peak, NEG)
    denom[...] = jnp.zeros_like(denom)
    numer[...] = jnp.zeros_like(numer)

    def first(b, t):
        at = pl.ds(pl.multiple_of(t * BLOCK, BLOCK), BLOCK)
        values = score(rows_ref, tgt_ref, b, t) * INV + crow[:, at]
        q[b * columns + t] = values
        peak[b] = functools.reduce(jnp.maximum, lane_parts(values), peak[b])

    tiles(live_ref, first)
    tops = []
    for b in range(blocks):
        tops.append(jnp.max(peak[b].T, axis=0, keepdims=True))
        peak[b] = jnp.broadcast_to(jnp.max(peak[b], axis=1, keepdims=True), peak[b].shape)

    def second(b, t):
        at = pl.ds(pl.multiple_of(t * BLOCK, BLOCK), BLOCK)
        top = jnp.concatenate([peak[b]] * (BLOCK // LANES), axis=1)
        weights = jnp.exp(q[b * columns + t] - top).astype(BF16)
        denom[b] = denom[b] + sum(lane_parts(weights.astype(F32)))
        numer[b] = numer[b] + lax.dot_general(tgt_ref[:, at], weights, NT, preferred_element_type=F32)

    tiles(live_ref, second)
    part = width // GROUPS
    chunk = out_ref.shape[2]
    for b in range(blocks):
        mass = jnp.sum(denom[b].T, axis=0, keepdims=True)
        inverse = 1.0 / jnp.where(mass > 0.0, mass, 1.0)
        logs = three_parts(safe_log(tops[b], mass))
        for k in range(GROUPS):
            buf[:part, :] = numer[b, k * part : (k + 1) * part, :] * inverse
            for j in range(3):
                buf[part + j : part + j + 1, :] = logs[j]
            buf[part + 3 :, :] = jnp.zeros_like(buf[part + 3 :, :])
            for r in range(BLOCK // chunk):
                place = (b * (BLOCK // chunk) + r) * GROUPS + k
                out_ref[place] = buf[:, r * chunk : (r + 1) * chunk].astype(BF16)


def merge_kernel(part, in_ref, out_ref, logs, buf):
    count = in_ref.shape[0]
    for t in range(count):
        tail = in_ref[t].astype(F32)
        logs[t : t + 1, :] = tail[part : part + 1] + tail[part + 1 : part + 2] + tail[part + 2 : part + 3]
    top = jnp.max(logs[...], axis=0, keepdims=True)
    share = jnp.exp(logs[...] - top)
    mass = jnp.sum(share, axis=0, keepdims=True)
    logs[...] = share / mass
    acc = jnp.zeros(in_ref.shape[1:], F32)
    for t in range(count):
        acc = acc + in_ref[t].astype(F32) * logs[t : t + 1, :]
    buf[...] = acc
    for j, piece in enumerate(three_parts(top + jnp.log(mass))):
        buf[part + j : part + j + 1, :] = piece
    out_ref[...] = jnp.broadcast_to(buf[...].astype(BF16)[None], out_ref.shape)


def final_kernel(part, in_ref, f_ref, mapped_ref, mass_ref, buf):
    chunk = in_ref.shape[2]
    per = chunk // LANES
    for r in range(in_ref.shape[0] // GROUPS):
        for k in range(GROUPS):
            piece = in_ref[r * GROUPS + k].astype(F32)
            buf[k * part : (k + 1) * part, :] = piece[:part]
        mapped_ref[:, r * chunk : (r + 1) * chunk] = buf[: GROUPS * part, :].astype(BF16)
        total = piece[part : part + 1] + piece[part + 1 : part + 2] + piece[part + 2 : part + 3]
        for j in range(per):
            at = r * per + j
            own = f_ref[at : at + 1, :] * INV
            mass_ref[at : at + 1, :] = own + total[:, j * LANES : (j + 1) * LANES]


VMEM = pl.BlockSpec(memory_space=pltpu.VMEM)
SMEM = pl.BlockSpec(memory_space=pltpu.SMEM)
PARAMS = pltpu.CompilerParams(vmem_limit_bytes=40 * 1024 * 1024)


def call(kernel, out_shape, scratch, *args, scalars=0):
    specs = [SMEM] * scalars + [VMEM] * (len(args) - scalars)
    return pl.pallas_call(
        kernel,
        out_shape=out_shape,
        in_specs=specs,
        out_specs=jax.tree.map(lambda _: VMEM, out_shape),
        scratch_shapes=scratch,
        compiler_params=PARAMS,
    )(*args)


def local(src_emb, tgt_emb, g_init, log_src, log_tgt, cand_ids, cand_count):
    s_rows, width = src_emb.shape
    t_cols = tgt_emb.shape[0]
    blocks, columns = s_rows // BLOCK, t_cols // BLOCK
    n_tgt, n_src = lax.axis_size("tgt"), lax.axis_size("src")
    shape = jax.ShapeDtypeStruct
    vmem = pltpu.VMEM

    slot = lax.broadcasted_iota(jnp.int32, cand_ids.shape, 1)
    owned = lax.axis_index("tgt") * columns + lax.broadcasted_iota(jnp.int32, (1, 1, columns), 2)
    asked = (cand_ids[:, :, None] == owned) & (slot < cand_count[:, None])[:, :, None]
    live = jnp.max(asked.astype(jnp.int32), axis=1)

    src_t, tgt_t = src_emb.T, tgt_emb.T
    s_tile = (s_rows // LANES, LANES)
    t_tile = (t_cols // LANES, LANES)
    padded = -(-width // LANES) * LANES

    rows, lse = call(
        row_kernel,
        (shape((s_rows, padded), BF16), shape((n_tgt, *s_tile), F32)),
        [
            vmem((padded, s_rows), F32),
            vmem((blocks, BLOCK, LANES), F32),
            vmem((blocks, BLOCK, LANES), F32),
            vmem(s_tile, F32),
        ],
        live, src_t, tgt_t, g_init.reshape(1, t_cols),
        scalars=1,
    )
    lse = lax.all_to_all(lse, "tgt", 0, 0, tiled=True)
    f, lse = call(
        col_kernel,
        (shape(s_tile, F32), shape((n_src, *t_tile), F32)),
        [
            vmem((s_rows, LANES), F32),
            vmem((columns, 8, BLOCK), F32),
            vmem((columns, 8, BLOCK), F32),
            vmem(t_tile, F32),
        ],
        live, rows, tgt_t, lse, log_src.reshape(s_tile),
        scalars=1,
    )
    lse = lax.all_to_all(lse, "src", 0, 0, tiled=True)
    chunk = s_rows * GROUPS // n_tgt
    c, sums = call(
        map_kernel,
        (shape(t_tile, F32), shape((n_tgt, CHUNK, chunk), BF16)),
        [
            vmem((1, t_cols), F32),
            vmem((blocks * columns, BLOCK, BLOCK), F32),
            vmem((blocks, BLOCK, LANES), F32),
            vmem((blocks, BLOCK, LANES), F32),
            vmem((blocks, width, BLOCK), F32),
            vmem((CHUNK, BLOCK), F32),
        ],
        live, rows, tgt_t, lse, log_tgt.reshape(t_tile),
        scalars=1,
    )
    sums = lax.all_to_all(sums, "tgt", 0, 0, tiled=True)
    part = width // GROUPS
    sums = call(
        functools.partial(merge_kernel, part),
        shape((n_tgt, CHUNK, chunk), BF16),
        [vmem((n_tgt, chunk), F32), vmem((CHUNK, chunk), F32)],
        sums,
    )
    sums = lax.all_to_all(sums, "tgt", 0, 0, tiled=True)
    mapped, mass = call(
        functools.partial(final_kernel, part),
        (shape((width, s_rows), BF16), shape(s_tile, F32)),
        [vmem((-(-width // 8) * 8, chunk), F32)],
        sums, f,
    )
    return f.reshape(s_rows), c.reshape(t_cols), mapped.T, mass.reshape(s_rows)


def solution(mesh):
    return jax.shard_map(
        local,
        mesh=mesh,
        in_specs=(
            P("src", None),
            P("tgt", None),
            P("tgt"),
            P("src"),
            P("tgt"),
            P("src", None),
            P("src"),
        ),
        out_specs=(P("src"), P("tgt"), P("src", None), P("src")),
        check_vma=False,
    )
```

```python
import functools
import itertools

import jax
import jax.numpy as jnp
from jax import lax
from jax.experimental import pallas as pl
from jax.experimental.pallas import tpu as pltpu
from jax.sharding import PartitionSpec as P

BLOCK = 512
LANES = 128
EPS = 0.2
INV = 5.0
LN2 = 0.6931471805599453
SCALE = INV / LN2
STRIP = 32
NEG = -1e30
GROUPS = 4
CHUNK = 80
NT = (((1,), (1,)), ((), ()))
F32 = jnp.float32
BF16 = jnp.bfloat16


def logsum(values, axis):
    peak = jnp.max(values, axis=axis, keepdims=True)
    return peak + jnp.log(jnp.sum(jnp.exp(values - peak), axis=axis, keepdims=True))


def safe_log(peak, total):
    return jnp.where(total > 0.0, peak * LN2 + jnp.log(jnp.where(total > 0.0, total, 1.0)), NEG)


def lane_parts(tile):
    return [tile[:, k * LANES : (k + 1) * LANES] for k in range(tile.shape[1] // LANES)]


def three_parts(value):
    high = value.astype(BF16).astype(F32)
    rest = value - high
    middle = rest.astype(BF16).astype(F32)
    return high, middle, rest - middle


def pick(order_ref, i, columns):
    last = order_ref.shape[0] - 1
    place = order_ref[jnp.minimum(i, last - 1)]
    return place, place // columns, place % columns, i < order_ref[last]


def in_turn(order_ref, columns, make, use):
    tile = functools.partial(pick, order_ref, columns=columns)
    make(0, tile(0))

    def step(k, carry):
        i = 2 * k
        make(1, tile(i + 1))
        use(0, tile(i))
        make(0, tile(i + 2))
        use(1, tile(i + 1))
        return carry

    lax.fori_loop(0, (order_ref[order_ref.shape[0] - 1] + 1) // 2, step, 0)


def each(order_ref, columns, use):
    tile = functools.partial(pick, order_ref, columns=columns)

    def step(k, carry):
        use(tile(2 * k))
        use(tile(2 * k + 1))
        return carry

    lax.fori_loop(0, (order_ref[order_ref.shape[0] - 1] + 1) // 2, step, 0)


def block_of(index):
    return pl.ds(pl.multiple_of(index * BLOCK, BLOCK), BLOCK)


def row_kernel(
    first_ref, count_hbm, ids_hbm, src_hbm, tgt_hbm, g_hbm, log_src_hbm, log_tgt_hbm,
    scores_ref, out_ref, order_ref, log_src_ref, log_tgt_ref,
    count_ref, ids_ref, src_ref, tgt_ref, g_ref, pad, rows_ref, peak, total, packed, slot0, slot1, sems,
):
    pairs = (
        (count_hbm, count_ref), (ids_hbm, ids_ref), (src_hbm, src_ref), (tgt_hbm, tgt_ref),
        (g_hbm, g_ref), (log_src_hbm, log_src_ref), (log_tgt_hbm, log_tgt_ref),
    )
    copies = [pltpu.make_async_copy(x, y, sems.at[i]) for i, (x, y) in enumerate(pairs)]
    for copy in copies:
        copy.start()
    width, s_rows = src_ref.shape
    blocks, columns = s_rows // BLOCK, tgt_ref.shape[1] // BLOCK
    peak[...] = jnp.full_like(peak, NEG)
    total[...] = jnp.zeros_like(total)

    copies[0].wait()
    copies[1].wait()
    lane = lax.broadcasted_iota(jnp.int32, (1, ids_ref.shape[1]), 1)
    live = []
    for b in range(blocks):
        rel = jnp.where(lane < count_ref[b], ids_ref[b : b + 1, :] - first_ref[0], -1)
        for t in range(columns):
            live.append(jnp.max(jnp.where(rel == t, 1.0, 0.0)) > 0.0)
    count = jnp.int32(0)
    latest = jnp.int32(0)
    for place, there in enumerate(live):
        latest = jnp.where(there, place, latest)
        order_ref[count] = latest
        count = count + there.astype(jnp.int32)

    def fill(i, carry):
        order_ref[i] = latest
        return carry

    lax.fori_loop(count, blocks * columns, fill, 0)
    order_ref[blocks * columns] = count

    copies[2].wait()
    edge = width // 8 * 8
    pad[edge:, :] = jnp.zeros_like(pad[edge:, :])
    pad[:width, :] = src_ref[...].astype(F32)
    for k in range(s_rows // LANES):
        piece = pad[:, k * LANES : (k + 1) * LANES]
        rows_ref[k * LANES : (k + 1) * LANES, :] = piece.T.astype(BF16)
    for copy in copies[3:]:
        copy.wait()

    slots = (slot0, slot1)

    def make(n, tile):
        place, b, t, there = tile
        rows = rows_ref[block_of(b), :]
        slots[n][...] = jnp.dot(rows[:, :width], tgt_ref[:, block_of(t)], preferred_element_type=F32)

    def use(n, tile):
        place, b, t, there = tile
        g = jnp.where(there, g_ref[:, block_of(t)] * SCALE, 2 * NEG)
        for r in range(0, BLOCK, STRIP):
            at = slice(r, r + STRIP)
            values = slots[n][at, :]
            scores_ref[place, at, :] = values
            z = lane_parts(values * SCALE + g)
            old = peak[b, at, :]
            new = functools.reduce(jnp.maximum, z, old)
            peak[b, at, :] = new
            total[b, at, :] = total[b, at, :] * jnp.exp2(old - new) + sum(jnp.exp2(part - new) for part in z)

    in_turn(order_ref, columns, make, use)
    per_block = BLOCK // LANES
    for b in range(blocks):
        turned = peak[b].T
        top = jnp.max(turned, axis=0, keepdims=True)
        mass = jnp.sum(total[b].T * jnp.exp2(turned - top), axis=0, keepdims=True)
        for k, part in enumerate(lane_parts(safe_log(top, mass))):
            packed[b * per_block + k : b * per_block + k + 1, :] = part
    out_ref[...] = jnp.broadcast_to(packed[...][None], out_ref.shape)


def col_kernel(order_ref, scores_ref, lse_ref, log_ref, f_ref, out_ref, fcol, peak, total, packed, slot0, slot1):
    f = EPS * log_ref[...] - EPS * logsum(lse_ref[...], 0)[0]
    f_ref[...] = f
    for k in range(f.shape[0]):
        row = jnp.broadcast_to(f[k : k + 1, :] * SCALE, (LANES, LANES))
        fcol[k * LANES : (k + 1) * LANES, :] = row.T
    peak[...] = jnp.full_like(peak, NEG)
    total[...] = jnp.zeros_like(total)
    columns = peak.shape[0]

    def use(slot, tile):
        place, b, t, there = tile
        extra = jnp.where(there, 0.0, 2 * NEG)
        old = peak[t]
        tops = [old] * 2
        for n, r in enumerate(range(0, BLOCK, STRIP)):
            at = slice(r, r + STRIP)
            own = fcol[pl.ds(pl.multiple_of(b * BLOCK + r, STRIP), STRIP), :] + extra
            y = scores_ref[place, at, :] * SCALE + jnp.concatenate([own] * (BLOCK // LANES), axis=1)
            slot[at, :] = y
            tops[n % 2] = jnp.maximum(tops[n % 2], jnp.max(y.reshape(STRIP // 8, 8, BLOCK), axis=0))
        new = jnp.maximum(*tops)
        peak[t] = new
        sums = [total[t] * jnp.exp2(old - new), jnp.zeros_like(new)]
        for n, r in enumerate(range(0, BLOCK, STRIP)):
            y = slot[slice(r, r + STRIP), :].reshape(STRIP // 8, 8, BLOCK)
            sums[n % 2] = sums[n % 2] + jnp.sum(jnp.exp2(y - new[None]), axis=0)
        total[t] = sums[0] + sums[1]

    slots = itertools.cycle((slot0, slot1))
    each(order_ref, columns, lambda tile: use(next(slots), tile))
    per_block = BLOCK // LANES
    for t in range(columns):
        top = jnp.max(peak[t], axis=0, keepdims=True)
        mass = jnp.sum(total[t] * jnp.exp2(peak[t] - top), axis=0, keepdims=True)
        for k, part in enumerate(lane_parts(safe_log(top, mass))):
            packed[t * per_block + k : t * per_block + k + 1, :] = part
    out_ref[...] = jnp.broadcast_to(packed[...][None], out_ref.shape)


def map_kernel(
    order_ref, scores_ref, tgt_ref, lse_ref, log_ref, c_ref, out_ref,
    crow, peak, denom, numer, buf, part0, part1,
):
    width = tgt_ref.shape[0]
    c = EPS * log_ref[...] - EPS * logsum(lse_ref[...], 0)[0]
    c_ref[...] = c
    for k in range(c.shape[0]):
        crow[:, k * LANES : (k + 1) * LANES] = c[k : k + 1, :] * SCALE
    blocks, columns = peak.shape[0], tgt_ref.shape[1] // BLOCK
    peak[...] = jnp.full_like(peak, NEG)
    denom[...] = jnp.zeros_like(denom)
    numer[...] = jnp.zeros_like(numer)

    def first(tile):
        place, b, t, there = tile
        own = crow[:, block_of(t)]
        for r in range(0, BLOCK, STRIP):
            at = slice(r, r + STRIP)
            values = scores_ref[place, at, :] * SCALE + own
            peak[b, at, :] = functools.reduce(jnp.maximum, lane_parts(values), peak[b, at, :])

    each(order_ref, columns, first)
    tops = []
    for b in range(blocks):
        tops.append(jnp.max(peak[b].T, axis=0, keepdims=True))
        peak[b] = jnp.broadcast_to(jnp.max(peak[b], axis=1, keepdims=True), peak[b].shape)

    slots = (part0, part1)

    def weigh(n, tile):
        place, b, t, there = tile
        extra = jnp.where(there, 0.0, -NEG)
        own = crow[:, block_of(t)]
        for r in range(0, BLOCK, STRIP):
            at = slice(r, r + STRIP)
            top = peak[b, at, :] + extra
            values = scores_ref[place, at, :] * SCALE + own
            weights = [jnp.exp2(part - top).astype(BF16) for part in lane_parts(values)]
            slots[n][at, :] = jnp.concatenate(weights, axis=1)
            denom[b, at, :] = denom[b, at, :] + sum(part.astype(F32) for part in weights)

    def add(n, tile):
        place, b, t, there = tile
        numer[b] = numer[b] + lax.dot_general(tgt_ref[:, block_of(t)], slots[n][...], NT, preferred_element_type=F32)

    @pl.when(order_ref[order_ref.shape[0] - 1] > 0)
    def _():
        in_turn(order_ref, columns, weigh, add)

    part = width // GROUPS
    chunk = out_ref.shape[2]
    for b in range(blocks):
        mass = jnp.sum(denom[b].T, axis=0, keepdims=True)
        inverse = 1.0 / jnp.where(mass > 0.0, mass, 1.0)
        logs = three_parts(safe_log(tops[b], mass))
        for k in range(GROUPS):
            buf[:part, :] = numer[b, k * part : (k + 1) * part, :] * inverse
            for j in range(3):
                buf[part + j : part + j + 1, :] = logs[j]
            buf[part + 3 :, :] = jnp.zeros_like(buf[part + 3 :, :])
            for r in range(BLOCK // chunk):
                place = (b * (BLOCK // chunk) + r) * GROUPS + k
                out_ref[place] = buf[:, r * chunk : (r + 1) * chunk].astype(BF16)


def merge_kernel(part, in_ref, out_ref, logs, buf):
    count = in_ref.shape[0]
    for t in range(count):
        tail = in_ref[t].astype(F32)
        logs[t : t + 1, :] = tail[part : part + 1] + tail[part + 1 : part + 2] + tail[part + 2 : part + 3]
    top = jnp.max(logs[...], axis=0, keepdims=True)
    share = jnp.exp(logs[...] - top)
    mass = jnp.sum(share, axis=0, keepdims=True)
    logs[...] = share / mass
    acc = jnp.zeros(in_ref.shape[1:], F32)
    for t in range(count):
        acc = acc + in_ref[t].astype(F32) * logs[t : t + 1, :]
    buf[...] = acc
    for j, piece in enumerate(three_parts(top + jnp.log(mass))):
        buf[part + j : part + j + 1, :] = piece
    out_ref[...] = jnp.broadcast_to(buf[...].astype(BF16)[None], out_ref.shape)


def final_kernel(part, in_ref, f_ref, mapped_ref, mass_ref, buf):
    chunk = in_ref.shape[2]
    per = chunk // LANES
    for r in range(in_ref.shape[0] // GROUPS):
        for k in range(GROUPS):
            piece = in_ref[r * GROUPS + k].astype(F32)
            buf[k * part : (k + 1) * part, :] = piece[:part]
        mapped_ref[:, r * chunk : (r + 1) * chunk] = buf[: GROUPS * part, :].astype(BF16)
        total = piece[part : part + 1] + piece[part + 1 : part + 2] + piece[part + 2 : part + 3]
        for j in range(per):
            at = r * per + j
            own = f_ref[at : at + 1, :] * INV
            mass_ref[at : at + 1, :] = own + total[:, j * LANES : (j + 1) * LANES]


VMEM = pl.BlockSpec(memory_space=pltpu.VMEM)
SMEM = pl.BlockSpec(memory_space=pltpu.SMEM)
HBM = pl.BlockSpec(memory_space=pltpu.HBM)
PARAMS = pltpu.CompilerParams(vmem_limit_bytes=24 * 1024 * 1024)


def call(kernel, out_shape, scratch, specs, *args, outs=None):
    return pl.pallas_call(
        kernel,
        out_shape=out_shape,
        in_specs=specs,
        out_specs=jax.tree.map(lambda _: VMEM, out_shape) if outs is None else outs,
        scratch_shapes=scratch,
        compiler_params=PARAMS,
    )(*args)


def run_rows(first, count, ids, src_t, tgt_t, g, log_src, log_tgt, n_tgt):
    (width, s_rows), t_cols = src_t.shape, tgt_t.shape[1]
    blocks, columns = s_rows // BLOCK, t_cols // BLOCK
    padded = -(-width // LANES) * LANES
    s_tile = (s_rows // LANES, LANES)
    return call(
        row_kernel,
        (
            jax.ShapeDtypeStruct((blocks * columns, BLOCK, BLOCK), F32),
            jax.ShapeDtypeStruct((n_tgt, *s_tile), F32),
            jax.ShapeDtypeStruct((blocks * columns + 1,), jnp.int32),
            jax.ShapeDtypeStruct(log_src.shape, F32),
            jax.ShapeDtypeStruct(log_tgt.shape, F32),
        ),
        [
            pltpu.SMEM(count.shape, jnp.int32),
            pltpu.VMEM(ids.shape, jnp.int32),
            pltpu.VMEM(src_t.shape, BF16),
            pltpu.VMEM(tgt_t.shape, BF16),
            pltpu.VMEM(g.shape, F32),
            pltpu.VMEM((padded, s_rows), F32),
            pltpu.VMEM((s_rows, padded), BF16),
            pltpu.VMEM((blocks, BLOCK, LANES), F32),
            pltpu.VMEM((blocks, BLOCK, LANES), F32),
            pltpu.VMEM(s_tile, F32),
            pltpu.VMEM((BLOCK, BLOCK), F32),
            pltpu.VMEM((BLOCK, BLOCK), F32),
            pltpu.SemaphoreType.DMA((7,)),
        ],
        [SMEM] + [HBM] * 7,
        first, *(pltpu.with_memory_space_constraint(x, pltpu.HBM) for x in (count, ids, src_t, tgt_t, g, log_src, log_tgt)),
        outs=(VMEM, VMEM, SMEM, VMEM, VMEM),
    )


def run_cols(order, scores, lse, log_src, n_src, t_cols):
    s_tile, s_rows = log_src.shape, log_src.size
    t_tile, columns = (t_cols // LANES, LANES), t_cols // BLOCK
    return call(
        col_kernel,
        (jax.ShapeDtypeStruct(s_tile, F32), jax.ShapeDtypeStruct((n_src, *t_tile), F32)),
        [
            pltpu.VMEM((s_rows, LANES), F32),
            pltpu.VMEM((columns, 8, BLOCK), F32),
            pltpu.VMEM((columns, 8, BLOCK), F32),
            pltpu.VMEM(t_tile, F32),
            pltpu.VMEM((BLOCK, BLOCK), F32),
            pltpu.VMEM((BLOCK, BLOCK), F32),
        ],
        [SMEM, VMEM, VMEM, VMEM],
        order, scores, lse, log_src,
    )


def run_map(order, scores, tgt_t, lse, log_tgt, n_tgt, s_rows):
    t_tile, (width, t_cols) = log_tgt.shape, tgt_t.shape
    blocks, columns = s_rows // BLOCK, t_cols // BLOCK
    chunk = s_rows * GROUPS // n_tgt
    return call(
        map_kernel,
        (jax.ShapeDtypeStruct(t_tile, F32), jax.ShapeDtypeStruct((n_tgt, CHUNK, chunk), BF16)),
        [
            pltpu.VMEM((1, t_cols), F32),
            pltpu.VMEM((blocks, BLOCK, LANES), F32),
            pltpu.VMEM((blocks, BLOCK, LANES), F32),
            pltpu.VMEM((blocks, width, BLOCK), F32),
            pltpu.VMEM((CHUNK, BLOCK), F32),
            pltpu.VMEM((BLOCK, BLOCK), BF16),
            pltpu.VMEM((BLOCK, BLOCK), BF16),
        ],
        [SMEM, VMEM, VMEM, VMEM, VMEM],
        order, scores, tgt_t, lse, log_tgt,
    )


def local(src_emb, tgt_emb, g_init, log_src, log_tgt, cand_ids, cand_count):
    s_rows, width = src_emb.shape
    t_cols = tgt_emb.shape[0]
    n_tgt, n_src = lax.axis_size("tgt"), lax.axis_size("src")
    src_t, tgt_t = src_emb.T, tgt_emb.T
    s_tile = (s_rows // LANES, LANES)
    t_tile = (t_cols // LANES, LANES)
    first = (lax.axis_index("tgt") * (t_cols // BLOCK)).astype(jnp.int32).reshape(1)

    scores, lse, order, log_src, log_tgt = run_rows(
        first, cand_count, cand_ids, src_t, tgt_t, g_init.reshape(1, t_cols),
        log_src.reshape(s_tile), log_tgt.reshape(t_tile), n_tgt,
    )
    lse = lax.all_to_all(lse, "tgt", 0, 0, tiled=True)
    f, lse = run_cols(order, scores, lse, log_src, n_src, t_cols)
    lse = lax.all_to_all(lse, "src", 0, 0, tiled=True)
    c, sums = run_map(order, scores, tgt_t, lse, log_tgt, n_tgt, s_rows)
    sums = lax.all_to_all(sums, "tgt", 0, 0, tiled=True)
    part, chunk = width // GROUPS, sums.shape[2]
    sums = call(
        functools.partial(merge_kernel, part),
        jax.ShapeDtypeStruct(sums.shape, BF16),
        [pltpu.VMEM((n_tgt, chunk), F32), pltpu.VMEM((CHUNK, chunk), F32)],
        [VMEM],
        sums,
    )
    sums = lax.all_to_all(sums, "tgt", 0, 0, tiled=True)
    mapped, mass = call(
        functools.partial(final_kernel, part),
        (jax.ShapeDtypeStruct((width, s_rows), BF16), jax.ShapeDtypeStruct(s_tile, F32)),
        [pltpu.VMEM((-(-width // 8) * 8, chunk), F32)],
        [VMEM, VMEM],
        sums, f,
    )
    return f.reshape(s_rows), c.reshape(t_cols), mapped.T, mass.reshape(s_rows)


def solution(mesh):
    return jax.shard_map(
        local,
        mesh=mesh,
        in_specs=(
            P("src", None),
            P("tgt", None),
            P("tgt"),
            P("src"),
            P("tgt"),
            P("src", None),
            P("src"),
        ),
        out_specs=(P("src"), P("tgt"), P("src", None), P("src")),
        check_vma=False,
    )
```

```python
import functools
import itertools

import jax
import jax.numpy as jnp
from jax import lax
from jax.experimental import pallas as pl
from jax.experimental.pallas import tpu as pltpu
from jax.sharding import PartitionSpec as P

BLOCK = 512
LANES = 128
EPS = 0.2
INV = 5.0
LN2 = 0.6931471805599453
SCALE = INV / LN2
STRIP = 32
COUNT = 127
NEG = -1e30
GROUPS = 4
CHUNK = 80
NT = (((1,), (1,)), ((), ()))
F32 = jnp.float32
BF16 = jnp.bfloat16


def logsum(values, axis):
    peak = jnp.max(values, axis=axis, keepdims=True)
    return peak + jnp.log(jnp.sum(jnp.exp(values - peak), axis=axis, keepdims=True))


def safe_log(peak, total):
    return jnp.where(total > 0.0, peak * LN2 + jnp.log(jnp.where(total > 0.0, total, 1.0)), NEG)


def lane_parts(tile):
    return [tile[:, k * LANES : (k + 1) * LANES] for k in range(tile.shape[1] // LANES)]


def three_parts(value):
    high = value.astype(BF16).astype(F32)
    rest = value - high
    middle = rest.astype(BF16).astype(F32)
    return high, middle, rest - middle


def pick(order_ref, i, columns):
    place = order_ref[0, jnp.minimum(i, COUNT - 1)]
    return place, place // columns, place % columns, i < order_ref[0, COUNT]


def in_turn(order_ref, columns, make, use):
    tile = functools.partial(pick, order_ref, columns=columns)
    make(0, tile(0))

    def step(k, carry):
        i = 2 * k
        make(1, tile(i + 1))
        use(0, tile(i))
        make(0, tile(i + 2))
        use(1, tile(i + 1))
        return carry

    lax.fori_loop(0, (order_ref[0, COUNT] + 1) // 2, step, 0)


def each(order_ref, columns, use):
    tile = functools.partial(pick, order_ref, columns=columns)

    def step(k, carry):
        use(tile(2 * k))
        use(tile(2 * k + 1))
        return carry

    lax.fori_loop(0, (order_ref[0, COUNT] + 1) // 2, step, 0)


def my_place():
    return lax.axis_index("tgt").astype(jnp.int32)


def block_of(index):
    return pl.ds(pl.multiple_of(index * BLOCK, BLOCK), BLOCK)


def row_kernel(
    count_hbm, ids_hbm, src_hbm, tgt_hbm, g_hbm, log_src_hbm, log_tgt_hbm,
    scores_ref, out_ref, list_ref, log_src_ref, log_tgt_ref,
    order_ref, count_ref, ids_ref, src_ref, tgt_ref, g_ref, pad, rows_ref, peak, total, packed, slot0, slot1, sems,
):
    pairs = (
        (count_hbm, count_ref), (ids_hbm, ids_ref), (src_hbm, src_ref), (tgt_hbm, tgt_ref),
        (g_hbm, g_ref), (log_src_hbm, log_src_ref), (log_tgt_hbm, log_tgt_ref),
    )
    copies = [pltpu.make_async_copy(x, y, sems.at[i]) for i, (x, y) in enumerate(pairs)]
    for copy in copies:
        copy.start()
    width, s_rows = src_ref.shape
    blocks, columns = s_rows // BLOCK, tgt_ref.shape[1] // BLOCK
    peak[...] = jnp.full_like(peak, NEG)
    total[...] = jnp.zeros_like(total)

    copies[0].wait()
    copies[1].wait()
    first = my_place() * columns
    lane = lax.broadcasted_iota(jnp.int32, (1, ids_ref.shape[1]), 1)
    live = []
    for b in range(blocks):
        rel = jnp.where(lane < count_ref[b], ids_ref[b : b + 1, :] - first, -1)
        for t in range(columns):
            live.append(jnp.max(jnp.where(rel == t, 1.0, 0.0)) > 0.0)
    latest = jnp.int32(0)
    for place, there in enumerate(live):
        latest = jnp.where(there, place, latest)
    for i in range(len(live)):
        order_ref[0, i] = latest
    count = jnp.int32(0)
    column = lax.broadcasted_iota(jnp.int32, list_ref.shape, 1)
    listed = jnp.full(list_ref.shape, latest)
    for place, there in enumerate(live):
        value = jnp.where(there, place, latest)
        order_ref[0, count] = value
        listed = jnp.where(column == count, value, listed)
        count = count + there.astype(jnp.int32)
    order_ref[0, COUNT] = count
    listed = jnp.where(column == COUNT, count, listed)
    list_ref[...] = listed

    copies[2].wait()
    edge = width // 8 * 8
    pad[edge:, :] = jnp.zeros_like(pad[edge:, :])
    pad[:width, :] = src_ref[...].astype(F32)
    for k in range(s_rows // LANES):
        piece = pad[:, k * LANES : (k + 1) * LANES]
        rows_ref[k * LANES : (k + 1) * LANES, :] = piece.T.astype(BF16)
    for copy in copies[3:]:
        copy.wait()

    slots = (slot0, slot1)

    def make(n, tile):
        place, b, t, there = tile
        rows = rows_ref[block_of(b), :]
        slots[n][...] = jnp.dot(rows[:, :width], tgt_ref[:, block_of(t)], preferred_element_type=F32)

    def use(n, tile):
        place, b, t, there = tile
        g = jnp.where(there, g_ref[:, block_of(t)] * SCALE, 2 * NEG)
        for r in range(0, BLOCK, STRIP):
            at = slice(r, r + STRIP)
            values = slots[n][at, :]
            scores_ref[place, at, :] = values
            z = lane_parts(values * SCALE + g)
            old = peak[b, at, :]
            new = functools.reduce(jnp.maximum, z, old)
            peak[b, at, :] = new
            total[b, at, :] = total[b, at, :] * jnp.exp2(old - new) + sum(jnp.exp2(part - new) for part in z)

    in_turn(order_ref, columns, make, use)
    per_block = BLOCK // LANES
    for b in range(blocks):
        turned = peak[b].T
        top = jnp.max(turned, axis=0, keepdims=True)
        mass = jnp.sum(total[b].T * jnp.exp2(turned - top), axis=0, keepdims=True)
        for k, part in enumerate(lane_parts(safe_log(top, mass))):
            packed[b * per_block + k : b * per_block + k + 1, :] = part
    out_ref[...] = jnp.broadcast_to(packed[...][None], out_ref.shape)


def col_kernel(
    list_ref, scores_ref, lse_ref, log_ref, f_hbm, out_ref, order_ref, f_ref, fcol, peak, total, packed, slot0, slot1, sems
):
    listed = pltpu.make_async_copy(list_ref, order_ref, sems.at[0])
    listed.start()
    f = EPS * log_ref[...] - EPS * logsum(lse_ref[...], 0)[0]
    f_ref[...] = f
    kept = pltpu.make_async_copy(f_ref, f_hbm, sems.at[1])
    kept.start()
    for k in range(f.shape[0]):
        row = jnp.broadcast_to(f[k : k + 1, :] * SCALE, (LANES, LANES))
        fcol[k * LANES : (k + 1) * LANES, :] = row.T
    peak[...] = jnp.full_like(peak, NEG)
    total[...] = jnp.zeros_like(total)
    columns = peak.shape[0]

    def use(slot, tile):
        place, b, t, there = tile
        extra = jnp.where(there, 0.0, 2 * NEG)
        old = peak[t]
        tops = [old] * 2
        for n, r in enumerate(range(0, BLOCK, STRIP)):
            at = slice(r, r + STRIP)
            own = fcol[pl.ds(pl.multiple_of(b * BLOCK + r, STRIP), STRIP), :] + extra
            y = scores_ref[place, at, :] * SCALE + jnp.concatenate([own] * (BLOCK // LANES), axis=1)
            slot[at, :] = y
            tops[n % 2] = jnp.maximum(tops[n % 2], jnp.max(y.reshape(STRIP // 8, 8, BLOCK), axis=0))
        new = jnp.maximum(*tops)
        peak[t] = new
        sums = [total[t] * jnp.exp2(old - new), jnp.zeros_like(new)]
        for n, r in enumerate(range(0, BLOCK, STRIP)):
            y = slot[slice(r, r + STRIP), :].reshape(STRIP // 8, 8, BLOCK)
            sums[n % 2] = sums[n % 2] + jnp.sum(jnp.exp2(y - new[None]), axis=0)
        total[t] = sums[0] + sums[1]

    listed.wait()
    slots = itertools.cycle((slot0, slot1))
    each(order_ref, columns, lambda tile: use(next(slots), tile))
    per_block = BLOCK // LANES
    for t in range(columns):
        top = jnp.max(peak[t], axis=0, keepdims=True)
        mass = jnp.sum(total[t] * jnp.exp2(peak[t] - top), axis=0, keepdims=True)
        for k, part in enumerate(lane_parts(safe_log(top, mass))):
            packed[t * per_block + k : t * per_block + k + 1, :] = part
    out_ref[...] = jnp.broadcast_to(packed[...][None], out_ref.shape)
    kept.wait()


def map_kernel(
    list_ref, scores_ref, tgt_ref, lse_ref, log_ref, c_hbm, out_ref,
    order_ref, c_ref, crow, peak, denom, numer, buf, part0, part1, sems,
):
    width = tgt_ref.shape[0]
    listed = pltpu.make_async_copy(list_ref, order_ref, sems.at[0])
    listed.start()
    c = EPS * log_ref[...] - EPS * logsum(lse_ref[...], 0)[0]
    c_ref[...] = c
    kept = pltpu.make_async_copy(c_ref, c_hbm, sems.at[1])
    kept.start()
    for k in range(c.shape[0]):
        crow[:, k * LANES : (k + 1) * LANES] = c[k : k + 1, :] * SCALE
    blocks, columns = peak.shape[0], tgt_ref.shape[1] // BLOCK
    peak[...] = jnp.full_like(peak, NEG)
    denom[...] = jnp.zeros_like(denom)
    numer[...] = jnp.zeros_like(numer)

    def first(tile):
        place, b, t, there = tile
        own = crow[:, block_of(t)]
        for r in range(0, BLOCK, STRIP):
            at = slice(r, r + STRIP)
            values = scores_ref[place, at, :] * SCALE + own
            peak[b, at, :] = functools.reduce(jnp.maximum, lane_parts(values), peak[b, at, :])

    listed.wait()
    each(order_ref, columns, first)
    tops = []
    for b in range(blocks):
        tops.append(jnp.max(peak[b].T, axis=0, keepdims=True))
        peak[b] = jnp.broadcast_to(jnp.max(peak[b], axis=1, keepdims=True), peak[b].shape)

    slots = (part0, part1)

    def weigh(n, tile):
        place, b, t, there = tile
        extra = jnp.where(there, 0.0, -NEG)
        own = crow[:, block_of(t)]
        for r in range(0, BLOCK, STRIP):
            at = slice(r, r + STRIP)
            top = peak[b, at, :] + extra
            values = scores_ref[place, at, :] * SCALE + own
            weights = [jnp.exp2(part - top).astype(BF16) for part in lane_parts(values)]
            slots[n][at, :] = jnp.concatenate(weights, axis=1)
            denom[b, at, :] = denom[b, at, :] + sum(part.astype(F32) for part in weights)

    def add(n, tile):
        place, b, t, there = tile
        numer[b] = numer[b] + lax.dot_general(tgt_ref[:, block_of(t)], slots[n][...], NT, preferred_element_type=F32)

    @pl.when(order_ref[0, COUNT] > 0)
    def _():
        in_turn(order_ref, columns, weigh, add)

    part = width // GROUPS
    chunk = out_ref.shape[2]
    for b in range(blocks):
        mass = jnp.sum(denom[b].T, axis=0, keepdims=True)
        inverse = 1.0 / jnp.where(mass > 0.0, mass, 1.0)
        logs = three_parts(safe_log(tops[b], mass))
        for k in range(GROUPS):
            buf[:part, :] = numer[b, k * part : (k + 1) * part, :] * inverse
            for j in range(3):
                buf[part + j : part + j + 1, :] = logs[j]
            buf[part + 3 :, :] = jnp.zeros_like(buf[part + 3 :, :])
            for r in range(BLOCK // chunk):
                place = (b * (BLOCK // chunk) + r) * GROUPS + k
                out_ref[place] = buf[:, r * chunk : (r + 1) * chunk].astype(BF16)
    kept.wait()


def merge_kernel(part, in_ref, out_ref, logs, buf):
    count = in_ref.shape[0]
    for t in range(count):
        tail = in_ref[t].astype(F32)
        logs[t : t + 1, :] = tail[part : part + 1] + tail[part + 1 : part + 2] + tail[part + 2 : part + 3]
    top = jnp.max(logs[...], axis=0, keepdims=True)
    share = jnp.exp(logs[...] - top)
    mass = jnp.sum(share, axis=0, keepdims=True)
    logs[...] = share / mass
    acc = jnp.zeros(in_ref.shape[1:], F32)
    for t in range(count):
        acc = acc + in_ref[t].astype(F32) * logs[t : t + 1, :]
    buf[...] = acc
    for j, piece in enumerate(three_parts(top + jnp.log(mass))):
        buf[part + j : part + j + 1, :] = piece
    out_ref[...] = jnp.broadcast_to(buf[...].astype(BF16)[None], out_ref.shape)


def final_kernel(part, in_ref, f_ref, mapped_ref, mass_ref, buf):
    chunk = in_ref.shape[2]
    per = chunk // LANES
    for r in range(in_ref.shape[0] // GROUPS):
        for k in range(GROUPS):
            piece = in_ref[r * GROUPS + k].astype(F32)
            buf[k * part : (k + 1) * part, :] = piece[:part]
        mapped_ref[:, r * chunk : (r + 1) * chunk] = buf[: GROUPS * part, :].astype(BF16)
        total = piece[part : part + 1] + piece[part + 1 : part + 2] + piece[part + 2 : part + 3]
        for j in range(per):
            at = r * per + j
            own = f_ref[at : at + 1, :] * INV
            mass_ref[at : at + 1, :] = own + total[:, j * LANES : (j + 1) * LANES]


VMEM = pl.BlockSpec(memory_space=pltpu.VMEM)
HBM = pl.BlockSpec(memory_space=pltpu.HBM)
PARAMS = pltpu.CompilerParams(vmem_limit_bytes=24 * 1024 * 1024)


def call(kernel, out_shape, scratch, specs, *args, outs=None):
    return pl.pallas_call(
        kernel,
        out_shape=out_shape,
        in_specs=specs,
        out_specs=jax.tree.map(lambda _: VMEM, out_shape) if outs is None else outs,
        scratch_shapes=scratch,
        compiler_params=PARAMS,
    )(*args)


def run_rows(count, ids, src_t, tgt_t, g, log_src, log_tgt, n_tgt):
    (width, s_rows), t_cols = src_t.shape, tgt_t.shape[1]
    blocks, columns = s_rows // BLOCK, t_cols // BLOCK
    padded = -(-width // LANES) * LANES
    s_tile = (s_rows // LANES, LANES)
    return call(
        row_kernel,
        (
            jax.ShapeDtypeStruct((blocks * columns, BLOCK, BLOCK), F32),
            jax.ShapeDtypeStruct((n_tgt, *s_tile), F32),
            jax.ShapeDtypeStruct((1, LANES), jnp.int32),
            jax.ShapeDtypeStruct(log_src.shape, F32),
            jax.ShapeDtypeStruct(log_tgt.shape, F32),
        ),
        [
            pltpu.SMEM((1, LANES), jnp.int32),
            pltpu.SMEM(count.shape, jnp.int32),
            pltpu.VMEM(ids.shape, jnp.int32),
            pltpu.VMEM(src_t.shape, BF16),
            pltpu.VMEM(tgt_t.shape, BF16),
            pltpu.VMEM(g.shape, F32),
            pltpu.VMEM((padded, s_rows), F32),
            pltpu.VMEM((s_rows, padded), BF16),
            pltpu.VMEM((blocks, BLOCK, LANES), F32),
            pltpu.VMEM((blocks, BLOCK, LANES), F32),
            pltpu.VMEM(s_tile, F32),
            pltpu.VMEM((BLOCK, BLOCK), F32),
            pltpu.VMEM((BLOCK, BLOCK), F32),
            pltpu.SemaphoreType.DMA((7,)),
        ],
        [HBM] * 7,
        *(pltpu.with_memory_space_constraint(x, pltpu.HBM) for x in (count, ids, src_t, tgt_t, g, log_src, log_tgt)),
    )


def run_cols(order, scores, lse, log_src, n_src, t_cols):
    s_tile, s_rows = log_src.shape, log_src.size
    t_tile, columns = (t_cols // LANES, LANES), t_cols // BLOCK
    return call(
        col_kernel,
        (jax.ShapeDtypeStruct(s_tile, F32), jax.ShapeDtypeStruct((n_src, *t_tile), F32)),
        [
            pltpu.SMEM((1, LANES), jnp.int32),
            pltpu.VMEM(s_tile, F32),
            pltpu.VMEM((s_rows, LANES), F32),
            pltpu.VMEM((columns, 8, BLOCK), F32),
            pltpu.VMEM((columns, 8, BLOCK), F32),
            pltpu.VMEM(t_tile, F32),
            pltpu.VMEM((BLOCK, BLOCK), F32),
            pltpu.VMEM((BLOCK, BLOCK), F32),
            pltpu.SemaphoreType.DMA((2,)),
        ],
        [VMEM, VMEM, VMEM, VMEM],
        order, scores, lse, log_src,
        outs=(HBM, VMEM),
    )


def run_map(order, scores, tgt_t, lse, log_tgt, n_tgt, s_rows):
    t_tile, (width, t_cols) = log_tgt.shape, tgt_t.shape
    blocks, columns = s_rows // BLOCK, t_cols // BLOCK
    chunk = s_rows * GROUPS // n_tgt
    return call(
        map_kernel,
        (jax.ShapeDtypeStruct(t_tile, F32), jax.ShapeDtypeStruct((n_tgt, CHUNK, chunk), BF16)),
        [
            pltpu.SMEM((1, LANES), jnp.int32),
            pltpu.VMEM(t_tile, F32),
            pltpu.VMEM((1, t_cols), F32),
            pltpu.VMEM((blocks, BLOCK, LANES), F32),
            pltpu.VMEM((blocks, BLOCK, LANES), F32),
            pltpu.VMEM((blocks, width, BLOCK), F32),
            pltpu.VMEM((CHUNK, BLOCK), F32),
            pltpu.VMEM((BLOCK, BLOCK), BF16),
            pltpu.VMEM((BLOCK, BLOCK), BF16),
            pltpu.SemaphoreType.DMA((2,)),
        ],
        [VMEM, VMEM, VMEM, VMEM, VMEM],
        order, scores, tgt_t, lse, log_tgt,
        outs=(HBM, VMEM),
    )


def local(src_emb, tgt_emb, g_init, log_src, log_tgt, cand_ids, cand_count):
    s_rows, width = src_emb.shape
    t_cols = tgt_emb.shape[0]
    n_tgt, n_src = lax.axis_size("tgt"), lax.axis_size("src")
    src_t, tgt_t = src_emb.T, tgt_emb.T
    s_tile = (s_rows // LANES, LANES)
    t_tile = (t_cols // LANES, LANES)

    scores, lse, order, log_src, log_tgt = run_rows(
        cand_count, cand_ids, src_t, tgt_t, g_init.reshape(1, t_cols),
        log_src.reshape(s_tile), log_tgt.reshape(t_tile), n_tgt,
    )
    lse = lax.all_to_all(lse, "tgt", 0, 0, tiled=True)
    f, lse = run_cols(order, scores, lse, log_src, n_src, t_cols)
    lse = lax.all_to_all(lse, "src", 0, 0, tiled=True)
    c, sums = run_map(order, scores, tgt_t, lse, log_tgt, n_tgt, s_rows)
    sums = lax.all_to_all(sums, "tgt", 0, 0, tiled=True)
    part, chunk = width // GROUPS, sums.shape[2]
    sums = call(
        functools.partial(merge_kernel, part),
        jax.ShapeDtypeStruct(sums.shape, BF16),
        [pltpu.VMEM((n_tgt, chunk), F32), pltpu.VMEM((CHUNK, chunk), F32)],
        [VMEM],
        sums,
    )
    sums = lax.all_to_all(sums, "tgt", 0, 0, tiled=True)
    mapped, mass = call(
        functools.partial(final_kernel, part),
        (jax.ShapeDtypeStruct((width, s_rows), BF16), jax.ShapeDtypeStruct(s_tile, F32)),
        [pltpu.VMEM((-(-width // 8) * 8, chunk), F32)],
        [VMEM, VMEM],
        sums, f,
    )
    return f.reshape(s_rows), c.reshape(t_cols), mapped.T, mass.reshape(s_rows)


def solution(mesh):
    return jax.shard_map(
        local,
        mesh=mesh,
        in_specs=(
            P("src", None),
            P("tgt", None),
            P("tgt"),
            P("src"),
            P("tgt"),
            P("src", None),
            P("src"),
        ),
        out_specs=(P("src"), P("tgt"), P("src", None), P("src")),
        check_vma=False,
    )
```

```python
import functools
import itertools

import jax
import jax.numpy as jnp
from jax import lax
from jax.experimental import pallas as pl
from jax.experimental.pallas import tpu as pltpu
from jax.sharding import PartitionSpec as P

BLOCK = 512
LANES = 128
EPS = 0.2
INV = 5.0
LN2 = 0.6931471805599453
SCALE = INV / LN2
STRIP = 32
COUNT = 127
BY_COLUMN = 64
BY_ROW = 96
TINY = 1e-27
NEG = -1e30
GROUPS = 4
CHUNK = 80
NT = (((1,), (1,)), ((), ()))
F32 = jnp.float32
BF16 = jnp.bfloat16


def logsum(values, axis):
    peak = jnp.max(values, axis=axis, keepdims=True)
    return peak + jnp.log(jnp.sum(jnp.exp(values - peak), axis=axis, keepdims=True))


def safe_log(peak, total):
    return jnp.where(total > 0.0, peak * LN2 + jnp.log(jnp.where(total > 0.0, total, 1.0)), NEG)


def lane_parts(tile):
    return [tile[:, k * LANES : (k + 1) * LANES] for k in range(tile.shape[1] // LANES)]


def three_parts(value):
    high = value.astype(BF16).astype(F32)
    rest = value - high
    middle = rest.astype(BF16).astype(F32)
    return high, middle, rest - middle


def pick(order_ref, i, columns):
    place = order_ref[0, jnp.minimum(i, COUNT - 1)]
    return place, place // columns, place % columns, i < order_ref[0, COUNT]


def in_turn(order_ref, columns, make, use):
    tile = functools.partial(pick, order_ref, columns=columns)
    make(0, tile(0))

    def step(k, carry):
        i = 2 * k
        make(1, tile(i + 1))
        use(0, tile(i))
        make(0, tile(i + 2))
        use(1, tile(i + 1))
        return carry

    lax.fori_loop(0, (order_ref[0, COUNT] + 1) // 2, step, 0)


def each(order_ref, columns, use):
    tile = functools.partial(pick, order_ref, columns=columns)

    def step(k, carry):
        use(tile(2 * k))
        use(tile(2 * k + 1))
        return carry

    lax.fori_loop(0, (order_ref[0, COUNT] + 1) // 2, step, 0)


def my_place():
    return lax.axis_index("tgt").astype(jnp.int32)


def block_of(index):
    return pl.ds(pl.multiple_of(index * BLOCK, BLOCK), BLOCK)


def row_kernel(
    count_hbm, ids_hbm, src_hbm, tgt_hbm, g_hbm, log_src_hbm, log_tgt_hbm,
    scores_ref, out_ref, list_ref, log_src_ref, log_tgt_ref,
    order_ref, count_ref, ids_ref, src_ref, tgt_ref, g_ref, pad, rows_ref, peak, total, packed, slot0, slot1, sems,
):
    pairs = (
        (count_hbm, count_ref), (ids_hbm, ids_ref), (src_hbm, src_ref), (tgt_hbm, tgt_ref),
        (g_hbm, g_ref), (log_src_hbm, log_src_ref), (log_tgt_hbm, log_tgt_ref),
    )
    copies = [pltpu.make_async_copy(x, y, sems.at[i]) for i, (x, y) in enumerate(pairs)]
    for copy in copies:
        copy.start()
    width, s_rows = src_ref.shape
    blocks, columns = s_rows // BLOCK, tgt_ref.shape[1] // BLOCK
    peak[...] = jnp.full_like(peak, NEG)
    total[...] = jnp.zeros_like(total)

    copies[0].wait()
    copies[1].wait()
    first = my_place() * columns
    lane = lax.broadcasted_iota(jnp.int32, (1, ids_ref.shape[1]), 1)
    live = []
    for b in range(blocks):
        rel = jnp.where(lane < count_ref[b], ids_ref[b : b + 1, :] - first, -1)
        for t in range(columns):
            live.append(jnp.max(jnp.where(rel == t, 1.0, 0.0)) > 0.0)
    latest = jnp.int32(0)
    for place, there in enumerate(live):
        latest = jnp.where(there, place, latest)
    for i in range(len(live)):
        order_ref[0, i] = latest
    count = jnp.int32(0)
    column = lax.broadcasted_iota(jnp.int32, list_ref.shape, 1)
    listed = jnp.full(list_ref.shape, latest)
    for place, there in enumerate(live):
        value = jnp.where(there, place, latest)
        order_ref[0, count] = value
        listed = jnp.where(column == count, value, listed)
        count = count + there.astype(jnp.int32)
    order_ref[0, COUNT] = count
    listed = jnp.where(column == COUNT, count, listed)
    for t in range(columns):
        there = functools.reduce(jnp.logical_or, live[t::columns])
        listed = jnp.where(column == BY_COLUMN + t, there.astype(jnp.int32), listed)
    for b in range(blocks):
        there = functools.reduce(jnp.logical_or, live[b * columns : (b + 1) * columns])
        listed = jnp.where(column == BY_ROW + b, there.astype(jnp.int32), listed)
    list_ref[...] = listed

    copies[2].wait()
    edge = width // 8 * 8
    pad[edge:, :] = jnp.zeros_like(pad[edge:, :])
    pad[:width, :] = src_ref[...].astype(F32)
    for k in range(s_rows // LANES):
        piece = pad[:, k * LANES : (k + 1) * LANES]
        rows_ref[k * LANES : (k + 1) * LANES, :] = piece.T.astype(BF16)
    for copy in copies[3:]:
        copy.wait()

    slots = (slot0, slot1)

    def make(n, tile):
        place, b, t, there = tile
        rows = rows_ref[block_of(b), :]
        slots[n][...] = jnp.dot(rows[:, :width], tgt_ref[:, block_of(t)], preferred_element_type=F32)

    def use(n, tile):
        place, b, t, there = tile
        g = jnp.where(there, g_ref[:, block_of(t)] * SCALE, 2 * NEG)
        for r in range(0, BLOCK, STRIP):
            at = slice(r, r + STRIP)
            values = slots[n][at, :]
            scores_ref[place, at, :] = values
            z = lane_parts(values * SCALE + g)
            old = peak[b, at, :]
            new = functools.reduce(jnp.maximum, z, old)
            peak[b, at, :] = new
            total[b, at, :] = total[b, at, :] * jnp.exp2(old - new) + sum(jnp.exp2(part - new) for part in z)

    in_turn(order_ref, columns, make, use)
    per_block = BLOCK // LANES
    for b in range(blocks):
        turned = peak[b].T
        top = jnp.max(turned, axis=0, keepdims=True)
        mass = jnp.sum(total[b].T * jnp.exp2(turned - top), axis=0, keepdims=True)
        for k, part in enumerate(lane_parts(safe_log(top, mass))):
            packed[b * per_block + k : b * per_block + k + 1, :] = part
    out_ref[...] = jnp.broadcast_to(packed[...][None], out_ref.shape)


def too_small(order_ref, start, masses):
    kept = [jnp.where(order_ref[0, start + i] > 0, mass, 1.0) for i, mass in enumerate(masses)]
    return jnp.min(functools.reduce(jnp.minimum, kept)) < TINY


def col_kernel(
    list_ref, scores_ref, lse_ref, log_ref, f_hbm, fcol, out_ref, order_ref, f_ref, peak, total, packed, slot0, slot1, sems
):
    listed = pltpu.make_async_copy(list_ref, order_ref, sems.at[0])
    listed.start()
    f = EPS * log_ref[...] - EPS * logsum(lse_ref[...], 0)[0]
    f_ref[...] = f
    kept = pltpu.make_async_copy(f_ref, f_hbm, sems.at[1])
    kept.start()
    for k in range(f.shape[0]):
        row = jnp.broadcast_to(f[k : k + 1, :] * SCALE, (LANES, LANES))
        fcol[k * LANES : (k + 1) * LANES, :] = row.T
    total[...] = jnp.zeros_like(total)
    columns = peak.shape[0]
    per_block = BLOCK // LANES

    def logits(tile, r):
        place, b, t, there = tile
        extra = jnp.where(there, 0.0, 2 * NEG)
        own = fcol[pl.ds(pl.multiple_of(b * BLOCK + r, STRIP), STRIP), :] + extra
        return scores_ref[place, r : r + STRIP, :] * SCALE + jnp.concatenate([own] * per_block, axis=1)

    def by_eight(values):
        return values.reshape(STRIP // 8, 8, BLOCK)

    def use(tile):
        sums = [total[tile[2]], jnp.zeros((8, BLOCK), F32)]
        for i, r in enumerate(range(0, BLOCK, STRIP)):
            sums[i % 2] = sums[i % 2] + jnp.sum(by_eight(jnp.exp2(logits(tile, r))), axis=0)
        total[tile[2]] = sums[0] + sums[1]

    listed.wait()
    each(order_ref, columns, use)

    def pack(t, top, mass):
        for k, part in enumerate(lane_parts(safe_log(top, mass))):
            packed[t * per_block + k : t * per_block + k + 1, :] = part

    masses = [jnp.sum(total[t], axis=0, keepdims=True) for t in range(columns)]
    for t in range(columns):
        pack(t, 0.0, masses[t])

    @pl.when(too_small(order_ref, BY_COLUMN, masses))
    def _():
        peak[...] = jnp.full_like(peak, NEG)
        total[...] = jnp.zeros_like(total)

        def scaled(slot, tile):
            t = tile[2]
            old = peak[t]
            tops = [old] * 2
            for i, r in enumerate(range(0, BLOCK, STRIP)):
                y = logits(tile, r)
                slot[r : r + STRIP, :] = y
                tops[i % 2] = jnp.maximum(tops[i % 2], jnp.max(by_eight(y), axis=0))
            new = jnp.maximum(*tops)
            peak[t] = new
            sums = [total[t] * jnp.exp2(old - new), jnp.zeros_like(new)]
            for i, r in enumerate(range(0, BLOCK, STRIP)):
                y = by_eight(slot[r : r + STRIP, :])
                sums[i % 2] = sums[i % 2] + jnp.sum(jnp.exp2(y - new[None]), axis=0)
            total[t] = sums[0] + sums[1]

        slots = itertools.cycle((slot0, slot1))
        each(order_ref, columns, lambda tile: scaled(next(slots), tile))
        for t in range(columns):
            top = jnp.max(peak[t], axis=0, keepdims=True)
            pack(t, top, jnp.sum(total[t] * jnp.exp2(peak[t] - top), axis=0, keepdims=True))

    out_ref[...] = jnp.broadcast_to(packed[...][None], out_ref.shape)
    kept.wait()


def map_kernel(
    list_ref, scores_ref, tgt_ref, lse_ref, log_ref, fcol, c_hbm, out_ref,
    order_ref, c_ref, crow, peak, shift, tops, denom, numer, buf, part0, part1, sems,
):
    width = tgt_ref.shape[0]
    listed = pltpu.make_async_copy(list_ref, order_ref, sems.at[0])
    listed.start()
    c = EPS * log_ref[...] - EPS * logsum(lse_ref[...], 0)[0]
    c_ref[...] = c
    kept = pltpu.make_async_copy(c_ref, c_hbm, sems.at[1])
    kept.start()
    for k in range(c.shape[0]):
        crow[:, k * LANES : (k + 1) * LANES] = c[k : k + 1, :] * SCALE
    blocks, columns = peak.shape[0], tgt_ref.shape[1] // BLOCK
    slots = (part0, part1)

    def strip(b, r):
        return pl.ds(pl.multiple_of(b * BLOCK + r, STRIP), STRIP)

    def weigh(shift_ref, n, tile):
        place, b, t, there = tile
        extra = jnp.where(there, 0.0, 2 * NEG)
        own = crow[:, block_of(t)]
        for r in range(0, BLOCK, STRIP):
            at = slice(r, r + STRIP)
            moved = shift_ref[strip(b, r), :] + extra
            values = scores_ref[place, at, :] * SCALE + own
            weights = [jnp.exp2(part + moved).astype(BF16) for part in lane_parts(values)]
            slots[n][at, :] = jnp.concatenate(weights, axis=1)
            denom[b, at, :] = denom[b, at, :] + sum(part.astype(F32) for part in weights)

    def add(n, tile):
        place, b, t, there = tile
        numer[b] = numer[b] + lax.dot_general(tgt_ref[:, block_of(t)], slots[n][...], NT, preferred_element_type=F32)

    def totals(shift_ref):
        denom[...] = jnp.zeros_like(denom)
        numer[...] = jnp.zeros_like(numer)

        @pl.when(order_ref[0, COUNT] > 0)
        def _():
            in_turn(order_ref, columns, functools.partial(weigh, shift_ref), add)

    def masses():
        return [jnp.sum(denom[b].T, axis=0, keepdims=True) for b in range(blocks)]

    tops[...] = jnp.zeros_like(tops)
    listed.wait()
    totals(fcol)

    @pl.when(too_small(order_ref, BY_ROW, masses()))
    def _():
        peak[...] = jnp.full_like(peak, NEG)

        def first(tile):
            place, b, t, there = tile
            own = crow[:, block_of(t)]
            for r in range(0, BLOCK, STRIP):
                at = slice(r, r + STRIP)
                parts = [part + fcol[strip(b, r), :] for part in lane_parts(scores_ref[place, at, :] * SCALE + own)]
                peak[b, at, :] = functools.reduce(jnp.maximum, parts, peak[b, at, :])

        each(order_ref, columns, first)
        for b in range(blocks):
            rows = slice(b * BLOCK, (b + 1) * BLOCK)
            tops[b : b + 1, :] = jnp.max(peak[b].T, axis=0, keepdims=True)
            shift[rows, :] = fcol[rows, :] - jnp.max(peak[b], axis=1, keepdims=True)
        totals(shift)

    part = width // GROUPS
    chunk = out_ref.shape[2]
    for b, mass in enumerate(masses()):
        inverse = 1.0 / jnp.where(mass > 0.0, mass, 1.0)
        logs = three_parts(safe_log(tops[b : b + 1, :], mass))
        for k in range(GROUPS):
            buf[:part, :] = numer[b, k * part : (k + 1) * part, :] * inverse
            for j in range(3):
                buf[part + j : part + j + 1, :] = logs[j]
            buf[part + 3 :, :] = jnp.zeros_like(buf[part + 3 :, :])
            for r in range(BLOCK // chunk):
                place = (b * (BLOCK // chunk) + r) * GROUPS + k
                out_ref[place] = buf[:, r * chunk : (r + 1) * chunk].astype(BF16)
    kept.wait()


def merge_kernel(part, in_ref, out_ref, logs, buf):
    count = in_ref.shape[0]
    for t in range(count):
        tail = in_ref[t].astype(F32)
        logs[t : t + 1, :] = tail[part : part + 1] + tail[part + 1 : part + 2] + tail[part + 2 : part + 3]
    top = jnp.max(logs[...], axis=0, keepdims=True)
    share = jnp.exp(logs[...] - top)
    mass = jnp.sum(share, axis=0, keepdims=True)
    logs[...] = share / mass
    acc = jnp.zeros(in_ref.shape[1:], F32)
    for t in range(count):
        acc = acc + in_ref[t].astype(F32) * logs[t : t + 1, :]
    buf[...] = acc
    for j, piece in enumerate(three_parts(top + jnp.log(mass))):
        buf[part + j : part + j + 1, :] = piece
    out_ref[...] = jnp.broadcast_to(buf[...].astype(BF16)[None], out_ref.shape)


def final_kernel(part, in_ref, mapped_hbm, mass_ref, mapped, buf, sems):
    chunk = in_ref.shape[2]
    per = chunk // LANES
    count = in_ref.shape[0] // GROUPS
    copies = []
    for r in range(count):
        for k in range(GROUPS):
            piece = in_ref[r * GROUPS + k].astype(F32)
            buf[k * part : (k + 1) * part, :] = piece[:part]
        mapped[:, r * chunk : (r + 1) * chunk] = buf[: GROUPS * part, :].astype(BF16)
        total = piece[part : part + 1] + piece[part + 1 : part + 2] + piece[part + 2 : part + 3]
        for j in range(per):
            mass_ref[r * per + j : r * per + j + 1, :] = total[:, j * LANES : (j + 1) * LANES]
        if (r + 1) % (count // 2) == 0:
            n = len(copies)
            half = pl.ds(n * (count // 2) * chunk, (count // 2) * chunk)
            copies.append(pltpu.make_async_copy(mapped.at[:, half], mapped_hbm.at[:, half], sems.at[n]))
            copies[n].start()
    for copy in copies:
        copy.wait()


VMEM = pl.BlockSpec(memory_space=pltpu.VMEM)
HBM = pl.BlockSpec(memory_space=pltpu.HBM)
PARAMS = pltpu.CompilerParams(vmem_limit_bytes=24 * 1024 * 1024)


def call(kernel, out_shape, scratch, specs, *args, outs=None):
    return pl.pallas_call(
        kernel,
        out_shape=out_shape,
        in_specs=specs,
        out_specs=jax.tree.map(lambda _: VMEM, out_shape) if outs is None else outs,
        scratch_shapes=scratch,
        compiler_params=PARAMS,
    )(*args)


def run_rows(count, ids, src_t, tgt_t, g, log_src, log_tgt, n_tgt):
    (width, s_rows), t_cols = src_t.shape, tgt_t.shape[1]
    blocks, columns = s_rows // BLOCK, t_cols // BLOCK
    padded = -(-width // LANES) * LANES
    s_tile = (s_rows // LANES, LANES)
    return call(
        row_kernel,
        (
            jax.ShapeDtypeStruct((blocks * columns, BLOCK, BLOCK), F32),
            jax.ShapeDtypeStruct((n_tgt, *s_tile), F32),
            jax.ShapeDtypeStruct((1, LANES), jnp.int32),
            jax.ShapeDtypeStruct(log_src.shape, F32),
            jax.ShapeDtypeStruct(log_tgt.shape, F32),
        ),
        [
            pltpu.SMEM((1, LANES), jnp.int32),
            pltpu.SMEM(count.shape, jnp.int32),
            pltpu.VMEM(ids.shape, jnp.int32),
            pltpu.VMEM(src_t.shape, BF16),
            pltpu.VMEM(tgt_t.shape, BF16),
            pltpu.VMEM(g.shape, F32),
            pltpu.VMEM((padded, s_rows), F32),
            pltpu.VMEM((s_rows, padded), BF16),
            pltpu.VMEM((blocks, BLOCK, LANES), F32),
            pltpu.VMEM((blocks, BLOCK, LANES), F32),
            pltpu.VMEM(s_tile, F32),
            pltpu.VMEM((BLOCK, BLOCK), F32),
            pltpu.VMEM((BLOCK, BLOCK), F32),
            pltpu.SemaphoreType.DMA((7,)),
        ],
        [HBM] * 7,
        *(pltpu.with_memory_space_constraint(x, pltpu.HBM) for x in (count, ids, src_t, tgt_t, g, log_src, log_tgt)),
    )


def run_cols(order, scores, lse, log_src, n_src, t_cols):
    s_tile, s_rows = log_src.shape, log_src.size
    t_tile, columns = (t_cols // LANES, LANES), t_cols // BLOCK
    return call(
        col_kernel,
        (
            jax.ShapeDtypeStruct(s_tile, F32),
            jax.ShapeDtypeStruct((s_rows, LANES), F32),
            jax.ShapeDtypeStruct((n_src, *t_tile), F32),
        ),
        [
            pltpu.SMEM((1, LANES), jnp.int32),
            pltpu.VMEM(s_tile, F32),
            pltpu.VMEM((columns, 8, BLOCK), F32),
            pltpu.VMEM((columns, 8, BLOCK), F32),
            pltpu.VMEM(t_tile, F32),
            pltpu.VMEM((BLOCK, BLOCK), F32),
            pltpu.VMEM((BLOCK, BLOCK), F32),
            pltpu.SemaphoreType.DMA((2,)),
        ],
        [VMEM, VMEM, VMEM, VMEM],
        order, scores, lse, log_src,
        outs=(HBM, VMEM, VMEM),
    )


def run_map(order, scores, tgt_t, lse, log_tgt, fcol, n_tgt):
    s_rows = fcol.shape[0]
    t_tile, (width, t_cols) = log_tgt.shape, tgt_t.shape
    blocks, columns = s_rows // BLOCK, t_cols // BLOCK
    chunk = s_rows * GROUPS // n_tgt
    return call(
        map_kernel,
        (jax.ShapeDtypeStruct(t_tile, F32), jax.ShapeDtypeStruct((n_tgt, CHUNK, chunk), BF16)),
        [
            pltpu.SMEM((1, LANES), jnp.int32),
            pltpu.VMEM(t_tile, F32),
            pltpu.VMEM((1, t_cols), F32),
            pltpu.VMEM((blocks, BLOCK, LANES), F32),
            pltpu.VMEM(fcol.shape, F32),
            pltpu.VMEM((blocks, BLOCK), F32),
            pltpu.VMEM((blocks, BLOCK, LANES), F32),
            pltpu.VMEM((blocks, width, BLOCK), F32),
            pltpu.VMEM((CHUNK, BLOCK), F32),
            pltpu.VMEM((BLOCK, BLOCK), BF16),
            pltpu.VMEM((BLOCK, BLOCK), BF16),
            pltpu.SemaphoreType.DMA((2,)),
        ],
        [VMEM] * 6,
        order, scores, tgt_t, lse, log_tgt, fcol,
        outs=(HBM, VMEM),
    )


def local(src_emb, tgt_emb, g_init, log_src, log_tgt, cand_ids, cand_count):
    s_rows, width = src_emb.shape
    t_cols = tgt_emb.shape[0]
    n_tgt, n_src = lax.axis_size("tgt"), lax.axis_size("src")
    src_t, tgt_t = src_emb.T, tgt_emb.T
    s_tile = (s_rows // LANES, LANES)
    t_tile = (t_cols // LANES, LANES)

    scores, lse, order, log_src, log_tgt = run_rows(
        cand_count, cand_ids, src_t, tgt_t, g_init.reshape(1, t_cols),
        log_src.reshape(s_tile), log_tgt.reshape(t_tile), n_tgt,
    )
    lse = lax.all_to_all(lse, "tgt", 0, 0, tiled=True)
    f, fcol, lse = run_cols(order, scores, lse, log_src, n_src, t_cols)
    lse = lax.all_to_all(lse, "src", 0, 0, tiled=True)
    c, sums = run_map(order, scores, tgt_t, lse, log_tgt, fcol, n_tgt)
    sums = lax.all_to_all(sums, "tgt", 0, 0, tiled=True)
    part, chunk = width // GROUPS, sums.shape[2]
    sums = call(
        functools.partial(merge_kernel, part),
        jax.ShapeDtypeStruct(sums.shape, BF16),
        [pltpu.VMEM((n_tgt, chunk), F32), pltpu.VMEM((CHUNK, chunk), F32)],
        [VMEM],
        sums,
    )
    sums = lax.all_to_all(sums, "tgt", 0, 0, tiled=True)
    mapped, mass = call(
        functools.partial(final_kernel, part),
        (jax.ShapeDtypeStruct((width, s_rows), BF16), jax.ShapeDtypeStruct(s_tile, F32)),
        [
            pltpu.VMEM((width, s_rows), BF16),
            pltpu.VMEM((-(-width // 8) * 8, chunk), F32),
            pltpu.SemaphoreType.DMA((2,)),
        ],
        [VMEM],
        sums,
        outs=(HBM, VMEM),
    )
    return f.reshape(s_rows), c.reshape(t_cols), mapped.T, mass.reshape(s_rows)


def solution(mesh):
    return jax.shard_map(
        local,
        mesh=mesh,
        in_specs=(
            P("src", None),
            P("tgt", None),
            P("tgt"),
            P("src"),
            P("tgt"),
            P("src", None),
            P("src"),
        ),
        out_specs=(P("src"), P("tgt"), P("src", None), P("src")),
        check_vma=False,
    )
```

```python
import functools
import itertools

import jax
import jax.numpy as jnp
from jax import lax
from jax.experimental import pallas as pl
from jax.experimental.pallas import tpu as pltpu
from jax.sharding import PartitionSpec as P

BLOCK = 512
LANES = 128
EPS = 0.2
INV = 5.0
LN2 = 0.6931471805599453
SCALE = INV / LN2
STRIP = 32
PART = 512
COUNT = 127
BY_COLUMN = 64
BY_ROW = 96
TINY = 1e-27
NEG = -1e30
GROUPS = 4
CHUNK = 80
NT = (((1,), (1,)), ((), ()))
F32 = jnp.float32
BF16 = jnp.bfloat16


def logsum(values, axis):
    peak = jnp.max(values, axis=axis, keepdims=True)
    return peak + jnp.log(jnp.sum(jnp.exp(values - peak), axis=axis, keepdims=True))


def safe_log(peak, total):
    return jnp.where(total > 0.0, peak * LN2 + jnp.log(jnp.where(total > 0.0, total, 1.0)), NEG)


def lane_parts(tile):
    return [tile[:, k * LANES : (k + 1) * LANES] for k in range(tile.shape[1] // LANES)]


def three_parts(value):
    high = value.astype(BF16).astype(F32)
    rest = value - high
    middle = rest.astype(BF16).astype(F32)
    return high, middle, rest - middle


def pick(order_ref, i, columns):
    place = order_ref[0, jnp.minimum(i, COUNT - 1)]
    return place, place // columns, place % columns, i < order_ref[0, COUNT]


def in_turn(order_ref, columns, make, use):
    tile = functools.partial(pick, order_ref, columns=columns)
    starts = range(0, BLOCK, PART)
    for start in starts:
        make(0, tile(0), start)

    def step(k, carry):
        i = 2 * k
        for start in starts:
            make(1, tile(i + 1), start)
            use(0, tile(i), start)
        for start in starts:
            make(0, tile(i + 2), start)
            use(1, tile(i + 1), start)
        return carry

    lax.fori_loop(0, (order_ref[0, COUNT] + 1) // 2, step, 0)


def each(order_ref, columns, use):
    tile = functools.partial(pick, order_ref, columns=columns)

    def step(k, carry):
        use(tile(2 * k))
        use(tile(2 * k + 1))
        return carry

    lax.fori_loop(0, (order_ref[0, COUNT] + 1) // 2, step, 0)


def my_place():
    return lax.axis_index("tgt").astype(jnp.int32)


def block_of(index):
    return pl.ds(pl.multiple_of(index * BLOCK, BLOCK), BLOCK)


def row_kernel(
    count_hbm, ids_hbm, src_hbm, tgt_hbm, g_hbm, log_src_hbm, log_tgt_hbm,
    scores_ref, out_ref, list_ref, log_src_ref, log_tgt_ref,
    order_ref, count_ref, ids_ref, src_ref, tgt_ref, g_ref, pad, rows_ref, peak, total, packed, slot0, slot1, sems,
):
    pairs = (
        (count_hbm, count_ref), (ids_hbm, ids_ref), (src_hbm, src_ref), (tgt_hbm, tgt_ref),
        (g_hbm, g_ref), (log_src_hbm, log_src_ref), (log_tgt_hbm, log_tgt_ref),
    )
    copies = [pltpu.make_async_copy(x, y, sems.at[i]) for i, (x, y) in enumerate(pairs)]
    for copy in copies:
        copy.start()
    width, s_rows = src_ref.shape
    blocks, columns = s_rows // BLOCK, tgt_ref.shape[1] // BLOCK
    peak[...] = jnp.full_like(peak, NEG)
    total[...] = jnp.zeros_like(total)

    copies[0].wait()
    copies[1].wait()
    first = my_place() * columns
    lane = lax.broadcasted_iota(jnp.int32, (1, ids_ref.shape[1]), 1)
    live = []
    for b in range(blocks):
        rel = jnp.where(lane < count_ref[b], ids_ref[b : b + 1, :] - first, -1)
        for t in range(columns):
            live.append(jnp.max(jnp.where(rel == t, 1.0, 0.0)) > 0.0)
    latest = jnp.int32(0)
    for place, there in enumerate(live):
        latest = jnp.where(there, place, latest)
    for i in range(len(live)):
        order_ref[0, i] = latest
    count = jnp.int32(0)
    column = lax.broadcasted_iota(jnp.int32, list_ref.shape, 1)
    listed = jnp.full(list_ref.shape, latest)
    for place, there in enumerate(live):
        value = jnp.where(there, place, latest)
        order_ref[0, count] = value
        listed = jnp.where(column == count, value, listed)
        count = count + there.astype(jnp.int32)
    order_ref[0, COUNT] = count
    listed = jnp.where(column == COUNT, count, listed)
    for t in range(columns):
        there = functools.reduce(jnp.logical_or, live[t::columns])
        listed = jnp.where(column == BY_COLUMN + t, there.astype(jnp.int32), listed)
    for b in range(blocks):
        there = functools.reduce(jnp.logical_or, live[b * columns : (b + 1) * columns])
        listed = jnp.where(column == BY_ROW + b, there.astype(jnp.int32), listed)
    list_ref[...] = listed

    copies[2].wait()
    edge = width // 8 * 8
    pad[edge:, :] = jnp.zeros_like(pad[edge:, :])
    pad[:width, :] = src_ref[...].astype(F32)
    for k in range(s_rows // LANES):
        piece = pad[:, k * LANES : (k + 1) * LANES]
        rows_ref[k * LANES : (k + 1) * LANES, :] = piece.T.astype(BF16)
    for copy in copies[3:]:
        copy.wait()

    slots = (slot0, slot1)

    def make(n, tile, start):
        place, b, t, there = tile
        at = slice(start, start + PART)
        rows = rows_ref[pl.ds(pl.multiple_of(b * BLOCK + start, PART), PART), :]
        values = jnp.dot(rows[:, :width], tgt_ref[:, block_of(t)], preferred_element_type=F32)
        slots[n][at, :] = values
        scores_ref[place, at, :] = values

    def use(n, tile, start):
        place, b, t, there = tile
        g = jnp.where(there, g_ref[:, block_of(t)] * SCALE, 2 * NEG)
        for r in range(start, start + PART, STRIP):
            at = slice(r, r + STRIP)
            z = lane_parts(slots[n][at, :] * SCALE + g)
            old = peak[b, at, :]
            new = functools.reduce(jnp.maximum, z, old)
            peak[b, at, :] = new
            total[b, at, :] = total[b, at, :] * jnp.exp2(old - new) + sum(jnp.exp2(part - new) for part in z)

    in_turn(order_ref, columns, make, use)
    per_block = BLOCK // LANES
    for b in range(blocks):
        turned = peak[b].T
        top = jnp.max(turned, axis=0, keepdims=True)
        mass = jnp.sum(total[b].T * jnp.exp2(turned - top), axis=0, keepdims=True)
        for k, part in enumerate(lane_parts(safe_log(top, mass))):
            packed[b * per_block + k : b * per_block + k + 1, :] = part
    out_ref[...] = jnp.broadcast_to(packed[...][None], out_ref.shape)


def too_small(order_ref, start, masses):
    kept = [jnp.where(order_ref[0, start + i] > 0, mass, 1.0) for i, mass in enumerate(masses)]
    return jnp.min(functools.reduce(jnp.minimum, kept)) < TINY


def col_kernel(
    list_ref, scores_ref, lse_ref, log_ref, f_hbm, fcol, out_ref, order_ref, f_ref, peak, total, packed, slot0, slot1, sems
):
    listed = pltpu.make_async_copy(list_ref, order_ref, sems.at[0])
    listed.start()
    f = EPS * log_ref[...] - EPS * logsum(lse_ref[...], 0)[0]
    f_ref[...] = f
    kept = pltpu.make_async_copy(f_ref, f_hbm, sems.at[1])
    kept.start()
    for k in range(f.shape[0]):
        row = jnp.broadcast_to(f[k : k + 1, :] * SCALE, (LANES, LANES))
        fcol[k * LANES : (k + 1) * LANES, :] = row.T
    total[...] = jnp.zeros_like(total)
    columns = peak.shape[0]
    per_block = BLOCK // LANES

    def logits(tile, r):
        place, b, t, there = tile
        extra = jnp.where(there, 0.0, 2 * NEG)
        own = fcol[pl.ds(pl.multiple_of(b * BLOCK + r, STRIP), STRIP), :] + extra
        return scores_ref[place, r : r + STRIP, :] * SCALE + jnp.concatenate([own] * per_block, axis=1)

    def by_eight(values):
        return values.reshape(STRIP // 8, 8, BLOCK)

    def use(tile):
        sums = [total[tile[2]], jnp.zeros((8, BLOCK), F32)]
        for i, r in enumerate(range(0, BLOCK, STRIP)):
            sums[i % 2] = sums[i % 2] + jnp.sum(by_eight(jnp.exp2(logits(tile, r))), axis=0)
        total[tile[2]] = sums[0] + sums[1]

    listed.wait()
    each(order_ref, columns, use)

    def pack(t, top, mass):
        for k, part in enumerate(lane_parts(safe_log(top, mass))):
            packed[t * per_block + k : t * per_block + k + 1, :] = part

    masses = [jnp.sum(total[t], axis=0, keepdims=True) for t in range(columns)]
    for t in range(columns):
        pack(t, 0.0, masses[t])

    @pl.when(too_small(order_ref, BY_COLUMN, masses))
    def _():
        peak[...] = jnp.full_like(peak, NEG)
        total[...] = jnp.zeros_like(total)

        def scaled(slot, tile):
            t = tile[2]
            old = peak[t]
            tops = [old] * 2
            for i, r in enumerate(range(0, BLOCK, STRIP)):
                y = logits(tile, r)
                slot[r : r + STRIP, :] = y
                tops[i % 2] = jnp.maximum(tops[i % 2], jnp.max(by_eight(y), axis=0))
            new = jnp.maximum(*tops)
            peak[t] = new
            sums = [total[t] * jnp.exp2(old - new), jnp.zeros_like(new)]
            for i, r in enumerate(range(0, BLOCK, STRIP)):
                y = by_eight(slot[r : r + STRIP, :])
                sums[i % 2] = sums[i % 2] + jnp.sum(jnp.exp2(y - new[None]), axis=0)
            total[t] = sums[0] + sums[1]

        slots = itertools.cycle((slot0, slot1))
        each(order_ref, columns, lambda tile: scaled(next(slots), tile))
        for t in range(columns):
            top = jnp.max(peak[t], axis=0, keepdims=True)
            pack(t, top, jnp.sum(total[t] * jnp.exp2(peak[t] - top), axis=0, keepdims=True))

    out_ref[...] = jnp.broadcast_to(packed[...][None], out_ref.shape)
    kept.wait()


def map_kernel(
    list_ref, scores_ref, tgt_ref, lse_ref, log_ref, fcol, c_hbm, out_ref,
    order_ref, c_ref, crow, peak, shift, tops, denom, numer, buf, part0, part1, sems,
):
    width = tgt_ref.shape[0]
    listed = pltpu.make_async_copy(list_ref, order_ref, sems.at[0])
    listed.start()
    c = EPS * log_ref[...] - EPS * logsum(lse_ref[...], 0)[0]
    c_ref[...] = c
    kept = pltpu.make_async_copy(c_ref, c_hbm, sems.at[1])
    kept.start()
    for k in range(c.shape[0]):
        crow[:, k * LANES : (k + 1) * LANES] = c[k : k + 1, :] * SCALE
    blocks, columns = peak.shape[0], tgt_ref.shape[1] // BLOCK
    slots = (part0, part1)

    def strip(b, r):
        return pl.ds(pl.multiple_of(b * BLOCK + r, STRIP), STRIP)

    def weigh(shift_ref, n, tile, start):
        place, b, t, there = tile
        extra = jnp.where(there, 0.0, 2 * NEG)
        own = crow[:, block_of(t)]
        for r in range(start, start + PART, STRIP):
            at = slice(r, r + STRIP)
            moved = shift_ref[strip(b, r), :] + extra
            values = scores_ref[place, at, :] * SCALE + own
            weights = [jnp.exp2(part + moved).astype(BF16) for part in lane_parts(values)]
            slots[n][at, :] = jnp.concatenate(weights, axis=1)
            denom[b, at, :] = denom[b, at, :] + sum(part.astype(F32) for part in weights)

    def add(n, tile, start):
        place, b, t, there = tile
        at = slice(start, start + PART)
        numer[b, :, at] = numer[b, :, at] + lax.dot_general(
            tgt_ref[:, block_of(t)], slots[n][at, :], NT, preferred_element_type=F32
        )

    def totals(shift_ref):
        denom[...] = jnp.zeros_like(denom)
        numer[...] = jnp.zeros_like(numer)

        @pl.when(order_ref[0, COUNT] > 0)
        def _():
            in_turn(order_ref, columns, functools.partial(weigh, shift_ref), add)

    def masses():
        return [jnp.sum(denom[b].T, axis=0, keepdims=True) for b in range(blocks)]

    tops[...] = jnp.zeros_like(tops)
    listed.wait()
    totals(fcol)

    @pl.when(too_small(order_ref, BY_ROW, masses()))
    def _():
        peak[...] = jnp.full_like(peak, NEG)

        def first(tile):
            place, b, t, there = tile
            own = crow[:, block_of(t)]
            for r in range(0, BLOCK, STRIP):
                at = slice(r, r + STRIP)
                parts = [part + fcol[strip(b, r), :] for part in lane_parts(scores_ref[place, at, :] * SCALE + own)]
                peak[b, at, :] = functools.reduce(jnp.maximum, parts, peak[b, at, :])

        each(order_ref, columns, first)
        for b in range(blocks):
            rows = slice(b * BLOCK, (b + 1) * BLOCK)
            tops[b : b + 1, :] = jnp.max(peak[b].T, axis=0, keepdims=True)
            shift[rows, :] = fcol[rows, :] - jnp.max(peak[b], axis=1, keepdims=True)
        totals(shift)

    part = width // GROUPS
    chunk = out_ref.shape[2]
    for b, mass in enumerate(masses()):
        inverse = 1.0 / jnp.where(mass > 0.0, mass, 1.0)
        logs = three_parts(safe_log(tops[b : b + 1, :], mass))
        for k in range(GROUPS):
            buf[:part, :] = numer[b, k * part : (k + 1) * part, :] * inverse
            for j in range(3):
                buf[part + j : part + j + 1, :] = logs[j]
            buf[part + 3 :, :] = jnp.zeros_like(buf[part + 3 :, :])
            for r in range(BLOCK // chunk):
                place = (b * (BLOCK // chunk) + r) * GROUPS + k
                out_ref[place] = buf[:, r * chunk : (r + 1) * chunk].astype(BF16)
    kept.wait()


def merge_kernel(part, in_ref, out_ref, logs, buf):
    count = in_ref.shape[0]
    for t in range(count):
        tail = in_ref[t].astype(F32)
        logs[t : t + 1, :] = tail[part : part + 1] + tail[part + 1 : part + 2] + tail[part + 2 : part + 3]
    top = jnp.max(logs[...], axis=0, keepdims=True)
    share = jnp.exp(logs[...] - top)
    mass = jnp.sum(share, axis=0, keepdims=True)
    logs[...] = share / mass
    acc = jnp.zeros(in_ref.shape[1:], F32)
    for t in range(count):
        acc = acc + in_ref[t].astype(F32) * logs[t : t + 1, :]
    buf[...] = acc
    for j, piece in enumerate(three_parts(top + jnp.log(mass))):
        buf[part + j : part + j + 1, :] = piece
    out_ref[...] = jnp.broadcast_to(buf[...].astype(BF16)[None], out_ref.shape)


def final_kernel(part, in_ref, mapped_ref, mass_ref, buf):
    chunk = in_ref.shape[2]
    per = chunk // LANES
    for r in range(in_ref.shape[0] // GROUPS):
        for k in range(GROUPS):
            piece = in_ref[r * GROUPS + k].astype(F32)
            buf[k * part : (k + 1) * part, :] = piece[:part]
        mapped_ref[:, r * chunk : (r + 1) * chunk] = buf[: GROUPS * part, :].astype(BF16)
        total = piece[part : part + 1] + piece[part + 1 : part + 2] + piece[part + 2 : part + 3]
        for j in range(per):
            mass_ref[r * per + j : r * per + j + 1, :] = total[:, j * LANES : (j + 1) * LANES]


VMEM = pl.BlockSpec(memory_space=pltpu.VMEM)
HBM = pl.BlockSpec(memory_space=pltpu.HBM)
PARAMS = pltpu.CompilerParams(vmem_limit_bytes=24 * 1024 * 1024)


def call(kernel, out_shape, scratch, specs, *args, outs=None):
    return pl.pallas_call(
        kernel,
        out_shape=out_shape,
        in_specs=specs,
        out_specs=jax.tree.map(lambda _: VMEM, out_shape) if outs is None else outs,
        scratch_shapes=scratch,
        compiler_params=PARAMS,
    )(*args)


def run_rows(count, ids, src_t, tgt_t, g, log_src, log_tgt, n_tgt):
    (width, s_rows), t_cols = src_t.shape, tgt_t.shape[1]
    blocks, columns = s_rows // BLOCK, t_cols // BLOCK
    padded = -(-width // LANES) * LANES
    s_tile = (s_rows // LANES, LANES)
    return call(
        row_kernel,
        (
            jax.ShapeDtypeStruct((blocks * columns, BLOCK, BLOCK), F32),
            jax.ShapeDtypeStruct((n_tgt, *s_tile), F32),
            jax.ShapeDtypeStruct((1, LANES), jnp.int32),
            jax.ShapeDtypeStruct(log_src.shape, F32),
            jax.ShapeDtypeStruct(log_tgt.shape, F32),
        ),
        [
            pltpu.SMEM((1, LANES), jnp.int32),
            pltpu.SMEM(count.shape, jnp.int32),
            pltpu.VMEM(ids.shape, jnp.int32),
            pltpu.VMEM(src_t.shape, BF16),
            pltpu.VMEM(tgt_t.shape, BF16),
            pltpu.VMEM(g.shape, F32),
            pltpu.VMEM((padded, s_rows), F32),
            pltpu.VMEM((s_rows, padded), BF16),
            pltpu.VMEM((blocks, BLOCK, LANES), F32),
            pltpu.VMEM((blocks, BLOCK, LANES), F32),
            pltpu.VMEM(s_tile, F32),
            pltpu.VMEM((BLOCK, BLOCK), F32),
            pltpu.VMEM((BLOCK, BLOCK), F32),
            pltpu.SemaphoreType.DMA((7,)),
        ],
        [HBM] * 7,
        *(pltpu.with_memory_space_constraint(x, pltpu.HBM) for x in (count, ids, src_t, tgt_t, g, log_src, log_tgt)),
    )


def run_cols(order, scores, lse, log_src, n_src, t_cols):
    s_tile, s_rows = log_src.shape, log_src.size
    t_tile, columns = (t_cols // LANES, LANES), t_cols // BLOCK
    return call(
        col_kernel,
        (
            jax.ShapeDtypeStruct(s_tile, F32),
            jax.ShapeDtypeStruct((s_rows, LANES), F32),
            jax.ShapeDtypeStruct((n_src, *t_tile), F32),
        ),
        [
            pltpu.SMEM((1, LANES), jnp.int32),
            pltpu.VMEM(s_tile, F32),
            pltpu.VMEM((columns, 8, BLOCK), F32),
            pltpu.VMEM((columns, 8, BLOCK), F32),
            pltpu.VMEM(t_tile, F32),
            pltpu.VMEM((BLOCK, BLOCK), F32),
            pltpu.VMEM((BLOCK, BLOCK), F32),
            pltpu.SemaphoreType.DMA((2,)),
        ],
        [VMEM, VMEM, VMEM, VMEM],
        order, scores, lse, log_src,
        outs=(HBM, VMEM, VMEM),
    )


def run_map(order, scores, tgt_t, lse, log_tgt, fcol, n_tgt):
    s_rows = fcol.shape[0]
    t_tile, (width, t_cols) = log_tgt.shape, tgt_t.shape
    blocks, columns = s_rows // BLOCK, t_cols // BLOCK
    chunk = s_rows * GROUPS // n_tgt
    return call(
        map_kernel,
        (jax.ShapeDtypeStruct(t_tile, F32), jax.ShapeDtypeStruct((n_tgt, CHUNK, chunk), BF16)),
        [
            pltpu.SMEM((1, LANES), jnp.int32),
            pltpu.VMEM(t_tile, F32),
            pltpu.VMEM((1, t_cols), F32),
            pltpu.VMEM((blocks, BLOCK, LANES), F32),
            pltpu.VMEM(fcol.shape, F32),
            pltpu.VMEM((blocks, BLOCK), F32),
            pltpu.VMEM((blocks, BLOCK, LANES), F32),
            pltpu.VMEM((blocks, width, BLOCK), F32),
            pltpu.VMEM((CHUNK, BLOCK), F32),
            pltpu.VMEM((BLOCK, BLOCK), BF16),
            pltpu.VMEM((BLOCK, BLOCK), BF16),
            pltpu.SemaphoreType.DMA((2,)),
        ],
        [VMEM] * 6,
        order, scores, tgt_t, lse, log_tgt, fcol,
        outs=(HBM, VMEM),
    )


def local(src_emb, tgt_emb, g_init, log_src, log_tgt, cand_ids, cand_count):
    s_rows, width = src_emb.shape
    t_cols = tgt_emb.shape[0]
    n_tgt, n_src = lax.axis_size("tgt"), lax.axis_size("src")
    src_t, tgt_t = src_emb.T, tgt_emb.T
    s_tile = (s_rows // LANES, LANES)
    t_tile = (t_cols // LANES, LANES)

    scores, lse, order, log_src, log_tgt = run_rows(
        cand_count, cand_ids, src_t, tgt_t, g_init.reshape(1, t_cols),
        log_src.reshape(s_tile), log_tgt.reshape(t_tile), n_tgt,
    )
    lse = lax.all_to_all(lse, "tgt", 0, 0, tiled=True)
    f, fcol, lse = run_cols(order, scores, lse, log_src, n_src, t_cols)
    lse = lax.all_to_all(lse, "src", 0, 0, tiled=True)
    c, sums = run_map(order, scores, tgt_t, lse, log_tgt, fcol, n_tgt)
    sums = lax.all_to_all(sums, "tgt", 0, 0, tiled=True)
    part, chunk = width // GROUPS, sums.shape[2]
    sums = call(
        functools.partial(merge_kernel, part),
        jax.ShapeDtypeStruct(sums.shape, BF16),
        [pltpu.VMEM((n_tgt, chunk), F32), pltpu.VMEM((CHUNK, chunk), F32)],
        [VMEM],
        sums,
    )
    sums = lax.all_to_all(sums, "tgt", 0, 0, tiled=True)
    mapped, mass = call(
        functools.partial(final_kernel, part),
        (jax.ShapeDtypeStruct((width, s_rows), BF16), jax.ShapeDtypeStruct(s_tile, F32)),
        [pltpu.VMEM((-(-width // 8) * 8, chunk), F32)],
        [VMEM],
        sums,
    )
    return f.reshape(s_rows), c.reshape(t_cols), mapped.T, mass.reshape(s_rows)


def solution(mesh):
    return jax.shard_map(
        local,
        mesh=mesh,
        in_specs=(
            P("src", None),
            P("tgt", None),
            P("tgt"),
            P("src"),
            P("tgt"),
            P("src", None),
            P("src"),
        ),
        out_specs=(P("src"), P("tgt"), P("src", None), P("src")),
        check_vma=False,
    )
```

```python
import functools
import itertools

import jax
import jax.numpy as jnp
from jax import lax
from jax.experimental import pallas as pl
from jax.experimental.pallas import tpu as pltpu
from jax.sharding import PartitionSpec as P

BLOCK = 512
LANES = 128
EPS = 0.2
INV = 5.0
LN2 = 0.6931471805599453
SCALE = INV / LN2
STRIP = 32
PART = 512
COUNT = 127
BY_COLUMN = 64
BY_ROW = 96
TINY = 1e-27
NEG = -1e30
GROUPS = 4
CHUNK = 80
NT = (((1,), (1,)), ((), ()))
F32 = jnp.float32
BF16 = jnp.bfloat16


def logsum(values, axis):
    peak = jnp.max(values, axis=axis, keepdims=True)
    return peak + jnp.log(jnp.sum(jnp.exp(values - peak), axis=axis, keepdims=True))


def safe_log(peak, total):
    return jnp.where(total > 0.0, peak * LN2 + jnp.log(jnp.where(total > 0.0, total, 1.0)), NEG)


def lane_parts(tile):
    return [tile[:, k * LANES : (k + 1) * LANES] for k in range(tile.shape[1] // LANES)]


def three_parts(value):
    high = value.astype(BF16).astype(F32)
    rest = value - high
    middle = rest.astype(BF16).astype(F32)
    return high, middle, rest - middle


def pick(order_ref, i, columns):
    place = order_ref[0, jnp.minimum(i, COUNT - 1)]
    return place, place // columns, place % columns, i < order_ref[0, COUNT]


def in_turn(order_ref, columns, make, use):
    tile = functools.partial(pick, order_ref, columns=columns)
    starts = range(0, BLOCK, PART)
    for start in starts:
        make(0, tile(0), start)

    def step(k, carry):
        i = 2 * k
        for start in starts:
            make(1, tile(i + 1), start)
            use(0, tile(i), start)
        for start in starts:
            make(0, tile(i + 2), start)
            use(1, tile(i + 1), start)
        return carry

    lax.fori_loop(0, (order_ref[0, COUNT] + 1) // 2, step, 0)


def each(order_ref, columns, use):
    tile = functools.partial(pick, order_ref, columns=columns)

    def step(k, carry):
        use(tile(2 * k))
        use(tile(2 * k + 1))
        return carry

    lax.fori_loop(0, (order_ref[0, COUNT] + 1) // 2, step, 0)


def my_place():
    return lax.axis_index("tgt").astype(jnp.int32)


def block_of(index):
    return pl.ds(pl.multiple_of(index * BLOCK, BLOCK), BLOCK)


def row_kernel(
    count_hbm, ids_hbm, src_hbm, tgt_hbm, g_hbm, log_src_hbm, log_tgt_hbm,
    scores_ref, out_ref, list_ref, log_src_ref, log_tgt_ref,
    order_ref, count_ref, ids_ref, src_ref, tgt_ref, g_ref, pad, rows_ref, peak, total, packed, slot0, slot1, sems,
):
    pairs = (
        (count_hbm, count_ref), (ids_hbm, ids_ref), (src_hbm, src_ref), (tgt_hbm, tgt_ref),
        (g_hbm, g_ref), (log_src_hbm, log_src_ref), (log_tgt_hbm, log_tgt_ref),
    )
    copies = [pltpu.make_async_copy(x, y, sems.at[i]) for i, (x, y) in enumerate(pairs)]
    for copy in copies:
        copy.start()
    width, s_rows = src_ref.shape
    blocks, columns = s_rows // BLOCK, tgt_ref.shape[1] // BLOCK
    peak[...] = jnp.full_like(peak, NEG)
    total[...] = jnp.zeros_like(total)

    copies[0].wait()
    copies[1].wait()
    first = my_place() * columns
    lane = lax.broadcasted_iota(jnp.int32, (1, ids_ref.shape[1]), 1)
    live = []
    for b in range(blocks):
        rel = jnp.where(lane < count_ref[b], ids_ref[b : b + 1, :] - first, -1)
        for t in range(columns):
            live.append(jnp.max(jnp.where(rel == t, 1.0, 0.0)) > 0.0)
    latest = jnp.int32(0)
    for place, there in enumerate(live):
        latest = jnp.where(there, place, latest)
    for i in range(len(live) + 2):
        order_ref[0, i] = latest
    count = jnp.int32(0)
    column = lax.broadcasted_iota(jnp.int32, list_ref.shape, 1)
    listed = jnp.full(list_ref.shape, latest)
    for place, there in enumerate(live):
        value = jnp.where(there, place, latest)
        order_ref[0, count] = value
        listed = jnp.where(column == count, value, listed)
        count = count + there.astype(jnp.int32)
    order_ref[0, COUNT] = count
    listed = jnp.where(column == COUNT, count, listed)
    for t in range(columns):
        there = functools.reduce(jnp.logical_or, live[t::columns])
        listed = jnp.where(column == BY_COLUMN + t, there.astype(jnp.int32), listed)
    for b in range(blocks):
        there = functools.reduce(jnp.logical_or, live[b * columns : (b + 1) * columns])
        listed = jnp.where(column == BY_ROW + b, there.astype(jnp.int32), listed)
    list_ref[...] = listed

    copies[2].wait()
    edge = width // 8 * 8
    pad[edge:, :] = jnp.zeros_like(pad[edge:, :])
    pad[:width, :] = src_ref[...].astype(F32)
    for k in range(s_rows // LANES):
        piece = pad[:, k * LANES : (k + 1) * LANES]
        rows_ref[k * LANES : (k + 1) * LANES, :] = piece.T.astype(BF16)
    for copy in copies[3:]:
        copy.wait()

    slots = (slot0, slot1)

    def make(n, tile, start):
        place, b, t, there = tile
        at = slice(start, start + PART)
        rows = rows_ref[pl.ds(pl.multiple_of(b * BLOCK + start, PART), PART), :]
        values = jnp.dot(rows[:, :width], tgt_ref[:, block_of(t)], preferred_element_type=F32)
        slots[n][at, :] = values
        scores_ref[place, at, :] = values

    def use(n, tile, start):
        place, b, t, there = tile
        g = jnp.where(there, g_ref[:, block_of(t)] * SCALE, 2 * NEG)
        for r in range(start, start + PART, STRIP):
            at = slice(r, r + STRIP)
            z = lane_parts(slots[n][at, :] * SCALE + g)
            old = peak[b, at, :]
            new = functools.reduce(jnp.maximum, z, old)
            peak[b, at, :] = new
            total[b, at, :] = total[b, at, :] * jnp.exp2(old - new) + sum(jnp.exp2(part - new) for part in z)

    in_turn(order_ref, columns, make, use)
    per_block = BLOCK // LANES
    for b in range(blocks):
        turned = peak[b].T
        top = jnp.max(turned, axis=0, keepdims=True)
        mass = jnp.sum(total[b].T * jnp.exp2(turned - top), axis=0, keepdims=True)
        for k, part in enumerate(lane_parts(safe_log(top, mass))):
            packed[b * per_block + k : b * per_block + k + 1, :] = part
    out_ref[...] = jnp.broadcast_to(packed[...][None], out_ref.shape)


def too_small(order_ref, start, masses):
    kept = [jnp.where(order_ref[0, start + i] > 0, mass, 1.0) for i, mass in enumerate(masses)]
    return jnp.min(functools.reduce(jnp.minimum, kept)) < TINY


def col_kernel(
    list_ref, scores_ref, lse_ref, log_ref, f_hbm, fcol, out_ref, order_ref, f_ref, peak, total, packed, slot0, slot1, sems
):
    listed = pltpu.make_async_copy(list_ref, order_ref, sems.at[0])
    listed.start()
    f = EPS * log_ref[...] - EPS * logsum(lse_ref[...], 0)[0]
    f_ref[...] = f
    kept = pltpu.make_async_copy(f_ref, f_hbm, sems.at[1])
    kept.start()
    for k in range(f.shape[0]):
        row = jnp.broadcast_to(f[k : k + 1, :] * SCALE, (LANES, LANES))
        fcol[k * LANES : (k + 1) * LANES, :] = row.T
    total[...] = jnp.zeros_like(total)
    columns = peak.shape[0]
    per_block = BLOCK // LANES

    def logits(tile, r):
        place, b, t, there = tile
        extra = jnp.where(there, 0.0, 2 * NEG)
        own = fcol[pl.ds(pl.multiple_of(b * BLOCK + r, STRIP), STRIP), :] + extra
        return scores_ref[place, r : r + STRIP, :] * SCALE + jnp.concatenate([own] * per_block, axis=1)

    def by_eight(values):
        return values.reshape(STRIP // 8, 8, BLOCK)

    def use(tile):
        sums = [total[tile[2]], jnp.zeros((8, BLOCK), F32)]
        for i, r in enumerate(range(0, BLOCK, STRIP)):
            sums[i % 2] = sums[i % 2] + jnp.sum(by_eight(jnp.exp2(logits(tile, r))), axis=0)
        total[tile[2]] = sums[0] + sums[1]

    listed.wait()
    each(order_ref, columns, use)

    def pack(t, top, mass):
        for k, part in enumerate(lane_parts(safe_log(top, mass))):
            packed[t * per_block + k : t * per_block + k + 1, :] = part

    masses = [jnp.sum(total[t], axis=0, keepdims=True) for t in range(columns)]
    for t in range(columns):
        pack(t, 0.0, masses[t])

    @pl.when(too_small(order_ref, BY_COLUMN, masses))
    def _():
        peak[...] = jnp.full_like(peak, NEG)
        total[...] = jnp.zeros_like(total)

        def scaled(slot, tile):
            t = tile[2]
            old = peak[t]
            tops = [old] * 2
            for i, r in enumerate(range(0, BLOCK, STRIP)):
                y = logits(tile, r)
                slot[r : r + STRIP, :] = y
                tops[i % 2] = jnp.maximum(tops[i % 2], jnp.max(by_eight(y), axis=0))
            new = jnp.maximum(*tops)
            peak[t] = new
            sums = [total[t] * jnp.exp2(old - new), jnp.zeros_like(new)]
            for i, r in enumerate(range(0, BLOCK, STRIP)):
                y = by_eight(slot[r : r + STRIP, :])
                sums[i % 2] = sums[i % 2] + jnp.sum(jnp.exp2(y - new[None]), axis=0)
            total[t] = sums[0] + sums[1]

        slots = itertools.cycle((slot0, slot1))
        each(order_ref, columns, lambda tile: scaled(next(slots), tile))
        for t in range(columns):
            top = jnp.max(peak[t], axis=0, keepdims=True)
            pack(t, top, jnp.sum(total[t] * jnp.exp2(peak[t] - top), axis=0, keepdims=True))

    out_ref[...] = jnp.broadcast_to(packed[...][None], out_ref.shape)
    kept.wait()


def map_kernel(
    list_ref, scores_ref, tgt_ref, lse_ref, log_ref, fcol, c_hbm, out_ref,
    order_ref, c_ref, crow, peak, shift, tops, mass_ref, denom, numer, buf, part0, part1, sems,
):
    width = tgt_ref.shape[0]
    listed = pltpu.make_async_copy(list_ref, order_ref, sems.at[0])
    listed.start()
    c = EPS * log_ref[...] - EPS * logsum(lse_ref[...], 0)[0]
    c_ref[...] = c
    kept = pltpu.make_async_copy(c_ref, c_hbm, sems.at[1])
    kept.start()
    for k in range(c.shape[0]):
        crow[:, k * LANES : (k + 1) * LANES] = c[k : k + 1, :] * SCALE
    blocks, columns = peak.shape[0], tgt_ref.shape[1] // BLOCK
    slots = (part0, part1)

    def strip(b, r):
        return pl.ds(pl.multiple_of(b * BLOCK + r, STRIP), STRIP)

    def weigh(shift_ref, n, tile, start):
        place, b, t, there = tile
        extra = jnp.where(there, 0.0, 2 * NEG)
        own = crow[:, block_of(t)]
        for r in range(start, start + PART, STRIP):
            at = slice(r, r + STRIP)
            moved = shift_ref[strip(b, r), :] + extra
            values = scores_ref[place, at, :] * SCALE + own
            weights = [jnp.exp2(part + moved).astype(BF16) for part in lane_parts(values)]
            slots[n][at, :] = jnp.concatenate(weights, axis=1)
            denom[b, at, :] = denom[b, at, :] + sum(part.astype(F32) for part in weights)

    def add(n, tile, start):
        place, b, t, there = tile
        at = slice(start, start + PART)
        numer[b, :, at] = numer[b, :, at] + lax.dot_general(
            tgt_ref[:, block_of(t)], slots[n][at, :], NT, preferred_element_type=F32
        )

    def totals(shift_ref):
        denom[...] = jnp.zeros_like(denom)
        numer[...] = jnp.zeros_like(numer)

        @pl.when(order_ref[0, COUNT] > 0)
        def _():
            in_turn(order_ref, columns, functools.partial(weigh, shift_ref), add)

        for b in range(blocks):
            mass_ref[b : b + 1, :] = jnp.sum(denom[b].T, axis=0, keepdims=True)

    def masses():
        return [mass_ref[b : b + 1, :] for b in range(blocks)]

    tops[...] = jnp.zeros_like(tops)
    listed.wait()
    totals(fcol)

    @pl.when(too_small(order_ref, BY_ROW, masses()))
    def _():
        peak[...] = jnp.full_like(peak, NEG)

        def first(tile):
            place, b, t, there = tile
            own = crow[:, block_of(t)]
            for r in range(0, BLOCK, STRIP):
                at = slice(r, r + STRIP)
                parts = [part + fcol[strip(b, r), :] for part in lane_parts(scores_ref[place, at, :] * SCALE + own)]
                peak[b, at, :] = functools.reduce(jnp.maximum, parts, peak[b, at, :])

        each(order_ref, columns, first)
        for b in range(blocks):
            rows = slice(b * BLOCK, (b + 1) * BLOCK)
            tops[b : b + 1, :] = jnp.max(peak[b].T, axis=0, keepdims=True)
            shift[rows, :] = fcol[rows, :] - jnp.max(peak[b], axis=1, keepdims=True)
        totals(shift)

    part = width // GROUPS
    chunk = out_ref.shape[2]
    for b, mass in enumerate(masses()):
        inverse = 1.0 / jnp.where(mass > 0.0, mass, 1.0)
        logs = three_parts(safe_log(tops[b : b + 1, :], mass))
        for k in range(GROUPS):
            buf[:part, :] = numer[b, k * part : (k + 1) * part, :] * inverse
            for j in range(3):
                buf[part + j : part + j + 1, :] = logs[j]
            buf[part + 3 :, :] = jnp.zeros_like(buf[part + 3 :, :])
            for r in range(BLOCK // chunk):
                place = (b * (BLOCK // chunk) + r) * GROUPS + k
                out_ref[place] = buf[:, r * chunk : (r + 1) * chunk].astype(BF16)
    kept.wait()


def merge_kernel(part, in_ref, out_ref, logs, buf):
    count = in_ref.shape[0]
    for t in range(count):
        tail = in_ref[t].astype(F32)
        logs[t : t + 1, :] = tail[part : part + 1] + tail[part + 1 : part + 2] + tail[part + 2 : part + 3]
    top = jnp.max(logs[...], axis=0, keepdims=True)
    share = jnp.exp(logs[...] - top)
    mass = jnp.sum(share, axis=0, keepdims=True)
    logs[...] = share / mass
    acc = jnp.zeros(in_ref.shape[1:], F32)
    for t in range(count):
        acc = acc + in_ref[t].astype(F32) * logs[t : t + 1, :]
    buf[...] = acc
    for j, piece in enumerate(three_parts(top + jnp.log(mass))):
        buf[part + j : part + j + 1, :] = piece
    out_ref[...] = jnp.broadcast_to(buf[...].astype(BF16)[None], out_ref.shape)


def final_kernel(part, in_ref, mapped_ref, mass_ref, buf):
    chunk = in_ref.shape[2]
    per = chunk // LANES
    for r in range(in_ref.shape[0] // GROUPS):
        for k in range(GROUPS):
            piece = in_ref[r * GROUPS + k].astype(F32)
            buf[k * part : (k + 1) * part, :] = piece[:part]
        mapped_ref[:, r * chunk : (r + 1) * chunk] = buf[: GROUPS * part, :].astype(BF16)
        total = piece[part : part + 1] + piece[part + 1 : part + 2] + piece[part + 2 : part + 3]
        for j in range(per):
            mass_ref[r * per + j : r * per + j + 1, :] = total[:, j * LANES : (j + 1) * LANES]


VMEM = pl.BlockSpec(memory_space=pltpu.VMEM)
HBM = pl.BlockSpec(memory_space=pltpu.HBM)
PARAMS = pltpu.CompilerParams(vmem_limit_bytes=24 * 1024 * 1024)


def call(kernel, out_shape, scratch, specs, *args, outs=None):
    return pl.pallas_call(
        kernel,
        out_shape=out_shape,
        in_specs=specs,
        out_specs=jax.tree.map(lambda _: VMEM, out_shape) if outs is None else outs,
        scratch_shapes=scratch,
        compiler_params=PARAMS,
    )(*args)


def run_rows(count, ids, src_t, tgt_t, g, log_src, log_tgt, n_tgt):
    (width, s_rows), t_cols = src_t.shape, tgt_t.shape[1]
    blocks, columns = s_rows // BLOCK, t_cols // BLOCK
    padded = -(-width // LANES) * LANES
    s_tile = (s_rows // LANES, LANES)
    return call(
        row_kernel,
        (
            jax.ShapeDtypeStruct((blocks * columns, BLOCK, BLOCK), F32),
            jax.ShapeDtypeStruct((n_tgt, *s_tile), F32),
            jax.ShapeDtypeStruct((1, LANES), jnp.int32),
            jax.ShapeDtypeStruct(log_src.shape, F32),
            jax.ShapeDtypeStruct(log_tgt.shape, F32),
        ),
        [
            pltpu.SMEM((1, LANES), jnp.int32),
            pltpu.SMEM(count.shape, jnp.int32),
            pltpu.VMEM(ids.shape, jnp.int32),
            pltpu.VMEM(src_t.shape, BF16),
            pltpu.VMEM(tgt_t.shape, BF16),
            pltpu.VMEM(g.shape, F32),
            pltpu.VMEM((padded, s_rows), F32),
            pltpu.VMEM((s_rows, padded), BF16),
            pltpu.VMEM((blocks, BLOCK, LANES), F32),
            pltpu.VMEM((blocks, BLOCK, LANES), F32),
            pltpu.VMEM(s_tile, F32),
            pltpu.VMEM((BLOCK, BLOCK), F32),
            pltpu.VMEM((BLOCK, BLOCK), F32),
            pltpu.SemaphoreType.DMA((7,)),
        ],
        [HBM] * 7,
        *(pltpu.with_memory_space_constraint(x, pltpu.HBM) for x in (count, ids, src_t, tgt_t, g, log_src, log_tgt)),
    )


def run_cols(order, scores, lse, log_src, n_src, t_cols):
    s_tile, s_rows = log_src.shape, log_src.size
    t_tile, columns = (t_cols // LANES, LANES), t_cols // BLOCK
    return call(
        col_kernel,
        (
            jax.ShapeDtypeStruct(s_tile, F32),
            jax.ShapeDtypeStruct((s_rows, LANES), F32),
            jax.ShapeDtypeStruct((n_src, *t_tile), F32),
        ),
        [
            pltpu.SMEM((1, LANES), jnp.int32),
            pltpu.VMEM(s_tile, F32),
            pltpu.VMEM((columns, 8, BLOCK), F32),
            pltpu.VMEM((columns, 8, BLOCK), F32),
            pltpu.VMEM(t_tile, F32),
            pltpu.VMEM((BLOCK, BLOCK), F32),
            pltpu.VMEM((BLOCK, BLOCK), F32),
            pltpu.SemaphoreType.DMA((2,)),
        ],
        [VMEM, VMEM, VMEM, VMEM],
        order, scores, lse, log_src,
        outs=(HBM, VMEM, VMEM),
    )


def run_map(order, scores, tgt_t, lse, log_tgt, fcol, n_tgt):
    s_rows = fcol.shape[0]
    t_tile, (width, t_cols) = log_tgt.shape, tgt_t.shape
    blocks, columns = s_rows // BLOCK, t_cols // BLOCK
    chunk = s_rows * GROUPS // n_tgt
    return call(
        map_kernel,
        (jax.ShapeDtypeStruct(t_tile, F32), jax.ShapeDtypeStruct((n_tgt, CHUNK, chunk), BF16)),
        [
            pltpu.SMEM((1, LANES), jnp.int32),
            pltpu.VMEM(t_tile, F32),
            pltpu.VMEM((1, t_cols), F32),
            pltpu.VMEM((blocks, BLOCK, LANES), F32),
            pltpu.VMEM(fcol.shape, F32),
            pltpu.VMEM((blocks, BLOCK), F32),
            pltpu.VMEM((blocks, BLOCK), F32),
            pltpu.VMEM((blocks, BLOCK, LANES), F32),
            pltpu.VMEM((blocks, width, BLOCK), F32),
            pltpu.VMEM((CHUNK, BLOCK), F32),
            pltpu.VMEM((BLOCK, BLOCK), BF16),
            pltpu.VMEM((BLOCK, BLOCK), BF16),
            pltpu.SemaphoreType.DMA((2,)),
        ],
        [VMEM] * 6,
        order, scores, tgt_t, lse, log_tgt, fcol,
        outs=(HBM, VMEM),
    )


def local(src_emb, tgt_emb, g_init, log_src, log_tgt, cand_ids, cand_count):
    s_rows, width = src_emb.shape
    t_cols = tgt_emb.shape[0]
    n_tgt, n_src = lax.axis_size("tgt"), lax.axis_size("src")
    src_t, tgt_t = src_emb.T, tgt_emb.T
    s_tile = (s_rows // LANES, LANES)
    t_tile = (t_cols // LANES, LANES)

    scores, lse, order, log_src, log_tgt = run_rows(
        cand_count, cand_ids, src_t, tgt_t, g_init.reshape(1, t_cols),
        log_src.reshape(s_tile), log_tgt.reshape(t_tile), n_tgt,
    )
    lse = lax.all_to_all(lse, "tgt", 0, 0, tiled=True)
    f, fcol, lse = run_cols(order, scores, lse, log_src, n_src, t_cols)
    lse = lax.all_to_all(lse, "src", 0, 0, tiled=True)
    c, sums = run_map(order, scores, tgt_t, lse, log_tgt, fcol, n_tgt)
    sums = lax.all_to_all(sums, "tgt", 0, 0, tiled=True)
    part, chunk = width // GROUPS, sums.shape[2]
    sums = call(
        functools.partial(merge_kernel, part),
        jax.ShapeDtypeStruct(sums.shape, BF16),
        [pltpu.VMEM((n_tgt, chunk), F32), pltpu.VMEM((CHUNK, chunk), F32)],
        [VMEM],
        sums,
    )
    sums = lax.all_to_all(sums, "tgt", 0, 0, tiled=True)
    mapped, mass = call(
        functools.partial(final_kernel, part),
        (jax.ShapeDtypeStruct((width, s_rows), BF16), jax.ShapeDtypeStruct(s_tile, F32)),
        [pltpu.VMEM((-(-width // 8) * 8, chunk), F32)],
        [VMEM],
        sums,
    )
    return f.reshape(s_rows), c.reshape(t_cols), mapped.T, mass.reshape(s_rows)


def solution(mesh):
    return jax.shard_map(
        local,
        mesh=mesh,
        in_specs=(
            P("src", None),
            P("tgt", None),
            P("tgt"),
            P("src"),
            P("tgt"),
            P("src", None),
            P("src"),
        ),
        out_specs=(P("src"), P("tgt"), P("src", None), P("src")),
        check_vma=False,
    )
```

```python
import functools
import itertools

import jax
import jax.numpy as jnp
from jax import lax
from jax.experimental import pallas as pl
from jax.experimental.pallas import tpu as pltpu
from jax.sharding import Mesh
from jax.sharding import PartitionSpec as P

BLOCK = 512
LANES = 128
EPS = 0.2
INV = 5.0
LN2 = 0.6931471805599453
SCALE = INV / LN2
STRIP = 32
PART = 512
COUNT = 127
BY_COLUMN = 64
BY_ROW = 96
TINY = 1e-27
NEG = -1e30
GROUPS = 4
CHUNK = 80
NT = (((1,), (1,)), ((), ()))
TGT = ("z", "x")
TURNED = ("x", "z")
F32 = jnp.float32
BF16 = jnp.bfloat16


def logsum(values, axis):
    peak = jnp.max(values, axis=axis, keepdims=True)
    return peak + jnp.log(jnp.sum(jnp.exp(values - peak), axis=axis, keepdims=True))


def safe_log(peak, total):
    return jnp.where(total > 0.0, peak * LN2 + jnp.log(jnp.where(total > 0.0, total, 1.0)), NEG)


def lane_parts(tile):
    return [tile[:, k * LANES : (k + 1) * LANES] for k in range(tile.shape[1] // LANES)]


def three_parts(value):
    high = value.astype(BF16).astype(F32)
    rest = value - high
    middle = rest.astype(BF16).astype(F32)
    return high, middle, rest - middle


def pick(order_ref, i, columns):
    place = order_ref[0, jnp.minimum(i, COUNT - 1)]
    return place, place // columns, place % columns, i < order_ref[0, COUNT]


def in_turn(order_ref, columns, make, use):
    tile = functools.partial(pick, order_ref, columns=columns)
    starts = range(0, BLOCK, PART)
    for start in starts:
        make(0, tile(0), start)

    def step(k, carry):
        i = 2 * k
        for start in starts:
            make(1, tile(i + 1), start)
            use(0, tile(i), start)
        for start in starts:
            make(0, tile(i + 2), start)
            use(1, tile(i + 1), start)
        return carry

    lax.fori_loop(0, (order_ref[0, COUNT] + 1) // 2, step, 0)


def each(order_ref, columns, use):
    tile = functools.partial(pick, order_ref, columns=columns)

    def step(k, carry):
        use(tile(2 * k))
        use(tile(2 * k + 1))
        return carry

    lax.fori_loop(0, (order_ref[0, COUNT] + 1) // 2, step, 0)


def my_place():
    return lax.axis_index(TGT).astype(jnp.int32)


def block_of(index):
    return pl.ds(pl.multiple_of(index * BLOCK, BLOCK), BLOCK)


def row_kernel(
    count_hbm, ids_hbm, src_hbm, tgt_hbm, g_hbm, log_src_hbm, log_tgt_hbm,
    scores_ref, out_ref, list_ref, log_src_ref, log_tgt_ref,
    order_ref, count_ref, ids_ref, src_ref, tgt_ref, g_ref, pad, rows_ref, peak, total, packed, slot0, slot1, sems,
):
    pairs = (
        (count_hbm, count_ref), (ids_hbm, ids_ref), (src_hbm, src_ref), (tgt_hbm, tgt_ref),
        (g_hbm, g_ref), (log_src_hbm, log_src_ref), (log_tgt_hbm, log_tgt_ref),
    )
    copies = [pltpu.make_async_copy(x, y, sems.at[i]) for i, (x, y) in enumerate(pairs)]
    for copy in copies:
        copy.start()
    width, s_rows = src_ref.shape
    blocks, columns = s_rows // BLOCK, tgt_ref.shape[1] // BLOCK
    peak[...] = jnp.full_like(peak, NEG)
    total[...] = jnp.zeros_like(total)

    copies[0].wait()
    copies[1].wait()
    first = my_place() * columns
    lane = lax.broadcasted_iota(jnp.int32, (1, ids_ref.shape[1]), 1)
    live = []
    for b in range(blocks):
        rel = jnp.where(lane < count_ref[b], ids_ref[b : b + 1, :] - first, -1)
        for t in range(columns):
            live.append(jnp.max(jnp.where(rel == t, 1.0, 0.0)) > 0.0)
    latest = jnp.int32(0)
    for place, there in enumerate(live):
        latest = jnp.where(there, place, latest)
    for i in range(len(live) + 2):
        order_ref[0, i] = latest
    count = jnp.int32(0)
    column = lax.broadcasted_iota(jnp.int32, list_ref.shape, 1)
    listed = jnp.full(list_ref.shape, latest)
    for place, there in enumerate(live):
        value = jnp.where(there, place, latest)
        order_ref[0, count] = value
        listed = jnp.where(column == count, value, listed)
        count = count + there.astype(jnp.int32)
    order_ref[0, COUNT] = count
    listed = jnp.where(column == COUNT, count, listed)
    for t in range(columns):
        there = functools.reduce(jnp.logical_or, live[t::columns])
        listed = jnp.where(column == BY_COLUMN + t, there.astype(jnp.int32), listed)
    for b in range(blocks):
        there = functools.reduce(jnp.logical_or, live[b * columns : (b + 1) * columns])
        listed = jnp.where(column == BY_ROW + b, there.astype(jnp.int32), listed)
    list_ref[...] = listed

    copies[2].wait()
    edge = width // 8 * 8
    pad[edge:, :] = jnp.zeros_like(pad[edge:, :])
    pad[:width, :] = src_ref[...].astype(F32)
    for k in range(s_rows // LANES):
        piece = pad[:, k * LANES : (k + 1) * LANES]
        rows_ref[k * LANES : (k + 1) * LANES, :] = piece.T.astype(BF16)
    for copy in copies[3:]:
        copy.wait()

    slots = (slot0, slot1)

    def make(n, tile, start):
        place, b, t, there = tile
        at = slice(start, start + PART)
        rows = rows_ref[pl.ds(pl.multiple_of(b * BLOCK + start, PART), PART), :]
        values = jnp.dot(rows[:, :width], tgt_ref[:, block_of(t)], preferred_element_type=F32)
        slots[n][at, :] = values
        scores_ref[place, at, :] = values

    def use(n, tile, start):
        place, b, t, there = tile
        g = jnp.where(there, g_ref[:, block_of(t)] * SCALE, 2 * NEG)
        for r in range(start, start + PART, STRIP):
            at = slice(r, r + STRIP)
            z = lane_parts(slots[n][at, :] * SCALE + g)
            old = peak[b, at, :]
            new = functools.reduce(jnp.maximum, z, old)
            peak[b, at, :] = new
            total[b, at, :] = total[b, at, :] * jnp.exp2(old - new) + sum(jnp.exp2(part - new) for part in z)

    in_turn(order_ref, columns, make, use)
    per_block = BLOCK // LANES
    for b in range(blocks):
        turned = peak[b].T
        top = jnp.max(turned, axis=0, keepdims=True)
        mass = jnp.sum(total[b].T * jnp.exp2(turned - top), axis=0, keepdims=True)
        for k, part in enumerate(lane_parts(safe_log(top, mass))):
            packed[b * per_block + k : b * per_block + k + 1, :] = part
    out_ref[...] = jnp.broadcast_to(packed[...][None], out_ref.shape)


def too_small(order_ref, start, masses):
    kept = [jnp.where(order_ref[0, start + i] > 0, mass, 1.0) for i, mass in enumerate(masses)]
    return jnp.min(functools.reduce(jnp.minimum, kept)) < TINY


def col_kernel(
    list_ref, scores_ref, lse_ref, log_ref, f_hbm, fcol, out_ref, order_ref, f_ref, peak, total, packed, slot0, slot1, sems
):
    listed = pltpu.make_async_copy(list_ref, order_ref, sems.at[0])
    listed.start()
    f = EPS * log_ref[...] - EPS * logsum(lse_ref[...], 0)[0]
    f_ref[...] = f
    kept = pltpu.make_async_copy(f_ref, f_hbm, sems.at[1])
    kept.start()
    for k in range(f.shape[0]):
        row = jnp.broadcast_to(f[k : k + 1, :] * SCALE, (LANES, LANES))
        fcol[k * LANES : (k + 1) * LANES, :] = row.T
    total[...] = jnp.zeros_like(total)
    columns = peak.shape[0]
    per_block = BLOCK // LANES

    def logits(tile, r):
        place, b, t, there = tile
        extra = jnp.where(there, 0.0, 2 * NEG)
        own = fcol[pl.ds(pl.multiple_of(b * BLOCK + r, STRIP), STRIP), :] + extra
        return scores_ref[place, r : r + STRIP, :] * SCALE + jnp.concatenate([own] * per_block, axis=1)

    def by_eight(values):
        return values.reshape(STRIP // 8, 8, BLOCK)

    def use(tile):
        sums = [total[tile[2]], jnp.zeros((8, BLOCK), F32)]
        for i, r in enumerate(range(0, BLOCK, STRIP)):
            sums[i % 2] = sums[i % 2] + jnp.sum(by_eight(jnp.exp2(logits(tile, r))), axis=0)
        total[tile[2]] = sums[0] + sums[1]

    listed.wait()
    each(order_ref, columns, use)

    def pack(t, top, mass):
        for k, part in enumerate(lane_parts(safe_log(top, mass))):
            packed[t * per_block + k : t * per_block + k + 1, :] = part

    masses = [jnp.sum(total[t], axis=0, keepdims=True) for t in range(columns)]
    for t in range(columns):
        pack(t, 0.0, masses[t])

    @pl.when(too_small(order_ref, BY_COLUMN, masses))
    def _():
        peak[...] = jnp.full_like(peak, NEG)
        total[...] = jnp.zeros_like(total)

        def scaled(slot, tile):
            t = tile[2]
            old = peak[t]
            tops = [old] * 2
            for i, r in enumerate(range(0, BLOCK, STRIP)):
                y = logits(tile, r)
                slot[r : r + STRIP, :] = y
                tops[i % 2] = jnp.maximum(tops[i % 2], jnp.max(by_eight(y), axis=0))
            new = jnp.maximum(*tops)
            peak[t] = new
            sums = [total[t] * jnp.exp2(old - new), jnp.zeros_like(new)]
            for i, r in enumerate(range(0, BLOCK, STRIP)):
                y = by_eight(slot[r : r + STRIP, :])
                sums[i % 2] = sums[i % 2] + jnp.sum(jnp.exp2(y - new[None]), axis=0)
            total[t] = sums[0] + sums[1]

        slots = itertools.cycle((slot0, slot1))
        each(order_ref, columns, lambda tile: scaled(next(slots), tile))
        for t in range(columns):
            top = jnp.max(peak[t], axis=0, keepdims=True)
            pack(t, top, jnp.sum(total[t] * jnp.exp2(peak[t] - top), axis=0, keepdims=True))

    out_ref[...] = jnp.broadcast_to(packed[...][None], out_ref.shape)
    kept.wait()


def map_kernel(
    list_ref, scores_ref, tgt_ref, lse_ref, log_ref, fcol, c_hbm, out_ref,
    order_ref, c_ref, crow, peak, shift, tops, mass_ref, denom, numer, buf, part0, part1, sems,
):
    width = tgt_ref.shape[0]
    listed = pltpu.make_async_copy(list_ref, order_ref, sems.at[0])
    listed.start()
    c = EPS * log_ref[...] - EPS * logsum(lse_ref[...], 0)[0]
    c_ref[...] = c
    kept = pltpu.make_async_copy(c_ref, c_hbm, sems.at[1])
    kept.start()
    for k in range(c.shape[0]):
        crow[:, k * LANES : (k + 1) * LANES] = c[k : k + 1, :] * SCALE
    blocks, columns = peak.shape[0], tgt_ref.shape[1] // BLOCK
    slots = (part0, part1)

    def strip(b, r):
        return pl.ds(pl.multiple_of(b * BLOCK + r, STRIP), STRIP)

    def weigh(shift_ref, n, tile, start):
        place, b, t, there = tile
        extra = jnp.where(there, 0.0, 2 * NEG)
        own = crow[:, block_of(t)]
        for r in range(start, start + PART, STRIP):
            at = slice(r, r + STRIP)
            moved = shift_ref[strip(b, r), :] + extra
            values = scores_ref[place, at, :] * SCALE + own
            weights = [jnp.exp2(part + moved).astype(BF16) for part in lane_parts(values)]
            slots[n][at, :] = jnp.concatenate(weights, axis=1)
            denom[b, at, :] = denom[b, at, :] + sum(part.astype(F32) for part in weights)

    def add(n, tile, start):
        place, b, t, there = tile
        at = slice(start, start + PART)
        numer[b, :, at] = numer[b, :, at] + lax.dot_general(
            tgt_ref[:, block_of(t)], slots[n][at, :], NT, preferred_element_type=F32
        )

    def totals(shift_ref):
        denom[...] = jnp.zeros_like(denom)
        numer[...] = jnp.zeros_like(numer)

        @pl.when(order_ref[0, COUNT] > 0)
        def _():
            in_turn(order_ref, columns, functools.partial(weigh, shift_ref), add)

        for b in range(blocks):
            mass_ref[b : b + 1, :] = jnp.sum(denom[b].T, axis=0, keepdims=True)

    def masses():
        return [mass_ref[b : b + 1, :] for b in range(blocks)]

    tops[...] = jnp.zeros_like(tops)
    listed.wait()
    totals(fcol)

    @pl.when(too_small(order_ref, BY_ROW, masses()))
    def _():
        peak[...] = jnp.full_like(peak, NEG)

        def first(tile):
            place, b, t, there = tile
            own = crow[:, block_of(t)]
            for r in range(0, BLOCK, STRIP):
                at = slice(r, r + STRIP)
                parts = [part + fcol[strip(b, r), :] for part in lane_parts(scores_ref[place, at, :] * SCALE + own)]
                peak[b, at, :] = functools.reduce(jnp.maximum, parts, peak[b, at, :])

        each(order_ref, columns, first)
        for b in range(blocks):
            rows = slice(b * BLOCK, (b + 1) * BLOCK)
            tops[b : b + 1, :] = jnp.max(peak[b].T, axis=0, keepdims=True)
            shift[rows, :] = fcol[rows, :] - jnp.max(peak[b], axis=1, keepdims=True)
        totals(shift)

    part = width // GROUPS
    chunk = out_ref.shape[2]
    for b, mass in enumerate(masses()):
        inverse = 1.0 / jnp.where(mass > 0.0, mass, 1.0)
        logs = three_parts(safe_log(tops[b : b + 1, :], mass))
        for k in range(GROUPS):
            buf[:part, :] = numer[b, k * part : (k + 1) * part, :] * inverse
            for j in range(3):
                buf[part + j : part + j + 1, :] = logs[j]
            buf[part + 3 :, :] = jnp.zeros_like(buf[part + 3 :, :])
            for r in range(BLOCK // chunk):
                place = (b * (BLOCK // chunk) + r) * GROUPS + k
                out_ref[place] = buf[:, r * chunk : (r + 1) * chunk].astype(BF16)
    kept.wait()


def merge_kernel(part, in_ref, out_ref, logs, buf):
    count = in_ref.shape[0]
    for t in range(count):
        tail = in_ref[t].astype(F32)
        logs[t : t + 1, :] = tail[part : part + 1] + tail[part + 1 : part + 2] + tail[part + 2 : part + 3]
    top = jnp.max(logs[...], axis=0, keepdims=True)
    share = jnp.exp(logs[...] - top)
    mass = jnp.sum(share, axis=0, keepdims=True)
    logs[...] = share / mass
    acc = jnp.zeros(in_ref.shape[1:], F32)
    for t in range(count):
        acc = acc + in_ref[t].astype(F32) * logs[t : t + 1, :]
    buf[...] = acc
    for j, piece in enumerate(three_parts(top + jnp.log(mass))):
        buf[part + j : part + j + 1, :] = piece
    out_ref[...] = jnp.broadcast_to(buf[...].astype(BF16)[None], out_ref.shape)


def final_kernel(part, in_ref, mapped_ref, mass_ref, buf):
    chunk = in_ref.shape[2]
    per = chunk // LANES
    for r in range(in_ref.shape[0] // GROUPS):
        for k in range(GROUPS):
            piece = in_ref[r * GROUPS + k].astype(F32)
            buf[k * part : (k + 1) * part, :] = piece[:part]
        mapped_ref[:, r * chunk : (r + 1) * chunk] = buf[: GROUPS * part, :].astype(BF16)
        total = piece[part : part + 1] + piece[part + 1 : part + 2] + piece[part + 2 : part + 3]
        for j in range(per):
            mass_ref[r * per + j : r * per + j + 1, :] = total[:, j * LANES : (j + 1) * LANES]


VMEM = pl.BlockSpec(memory_space=pltpu.VMEM)
HBM = pl.BlockSpec(memory_space=pltpu.HBM)
PARAMS = pltpu.CompilerParams(vmem_limit_bytes=24 * 1024 * 1024)


def call(kernel, out_shape, scratch, specs, *args, outs=None):
    return pl.pallas_call(
        kernel,
        out_shape=out_shape,
        in_specs=specs,
        out_specs=jax.tree.map(lambda _: VMEM, out_shape) if outs is None else outs,
        scratch_shapes=scratch,
        compiler_params=PARAMS,
    )(*args)


def run_rows(count, ids, src_t, tgt_t, g, log_src, log_tgt, n_tgt):
    (width, s_rows), t_cols = src_t.shape, tgt_t.shape[1]
    blocks, columns = s_rows // BLOCK, t_cols // BLOCK
    padded = -(-width // LANES) * LANES
    s_tile = (s_rows // LANES, LANES)
    return call(
        row_kernel,
        (
            jax.ShapeDtypeStruct((blocks * columns, BLOCK, BLOCK), F32),
            jax.ShapeDtypeStruct((n_tgt, *s_tile), F32),
            jax.ShapeDtypeStruct((1, LANES), jnp.int32),
            jax.ShapeDtypeStruct(log_src.shape, F32),
            jax.ShapeDtypeStruct(log_tgt.shape, F32),
        ),
        [
            pltpu.SMEM((1, LANES), jnp.int32),
            pltpu.SMEM(count.shape, jnp.int32),
            pltpu.VMEM(ids.shape, jnp.int32),
            pltpu.VMEM(src_t.shape, BF16),
            pltpu.VMEM(tgt_t.shape, BF16),
            pltpu.VMEM(g.shape, F32),
            pltpu.VMEM((padded, s_rows), F32),
            pltpu.VMEM((s_rows, padded), BF16),
            pltpu.VMEM((blocks, BLOCK, LANES), F32),
            pltpu.VMEM((blocks, BLOCK, LANES), F32),
            pltpu.VMEM(s_tile, F32),
            pltpu.VMEM((BLOCK, BLOCK), F32),
            pltpu.VMEM((BLOCK, BLOCK), F32),
            pltpu.SemaphoreType.DMA((7,)),
        ],
        [HBM] * 7,
        *(pltpu.with_memory_space_constraint(x, pltpu.HBM) for x in (count, ids, src_t, tgt_t, g, log_src, log_tgt)),
    )


def run_cols(order, scores, lse, log_src, n_src, t_cols):
    s_tile, s_rows = log_src.shape, log_src.size
    t_tile, columns = (t_cols // LANES, LANES), t_cols // BLOCK
    return call(
        col_kernel,
        (
            jax.ShapeDtypeStruct(s_tile, F32),
            jax.ShapeDtypeStruct((s_rows, LANES), F32),
            jax.ShapeDtypeStruct((n_src, *t_tile), F32),
        ),
        [
            pltpu.SMEM((1, LANES), jnp.int32),
            pltpu.VMEM(s_tile, F32),
            pltpu.VMEM((columns, 8, BLOCK), F32),
            pltpu.VMEM((columns, 8, BLOCK), F32),
            pltpu.VMEM(t_tile, F32),
            pltpu.VMEM((BLOCK, BLOCK), F32),
            pltpu.VMEM((BLOCK, BLOCK), F32),
            pltpu.SemaphoreType.DMA((2,)),
        ],
        [VMEM, VMEM, VMEM, VMEM],
        order, scores, lse, log_src,
        outs=(HBM, VMEM, VMEM),
    )


def run_map(order, scores, tgt_t, lse, log_tgt, fcol, n_tgt):
    s_rows = fcol.shape[0]
    t_tile, (width, t_cols) = log_tgt.shape, tgt_t.shape
    blocks, columns = s_rows // BLOCK, t_cols // BLOCK
    chunk = s_rows * GROUPS // n_tgt
    return call(
        map_kernel,
        (jax.ShapeDtypeStruct(t_tile, F32), jax.ShapeDtypeStruct((n_tgt, CHUNK, chunk), BF16)),
        [
            pltpu.SMEM((1, LANES), jnp.int32),
            pltpu.VMEM(t_tile, F32),
            pltpu.VMEM((1, t_cols), F32),
            pltpu.VMEM((blocks, BLOCK, LANES), F32),
            pltpu.VMEM(fcol.shape, F32),
            pltpu.VMEM((blocks, BLOCK), F32),
            pltpu.VMEM((blocks, BLOCK), F32),
            pltpu.VMEM((blocks, BLOCK, LANES), F32),
            pltpu.VMEM((blocks, width, BLOCK), F32),
            pltpu.VMEM((CHUNK, BLOCK), F32),
            pltpu.VMEM((BLOCK, BLOCK), BF16),
            pltpu.VMEM((BLOCK, BLOCK), BF16),
            pltpu.SemaphoreType.DMA((2,)),
        ],
        [VMEM] * 6,
        order, scores, tgt_t, lse, log_tgt, fcol,
        outs=(HBM, VMEM),
    )


def local(src_emb, tgt_emb, g_init, log_src, log_tgt, cand_ids, cand_count):
    s_rows, width = src_emb.shape
    t_cols = tgt_emb.shape[0]
    n_tgt, n_src = lax.axis_size(TGT), lax.axis_size("src")
    src_t, tgt_t = src_emb.T, tgt_emb.T
    s_tile = (s_rows // LANES, LANES)
    t_tile = (t_cols // LANES, LANES)

    scores, lse, order, log_src, log_tgt = run_rows(
        cand_count, cand_ids, src_t, tgt_t, g_init.reshape(1, t_cols),
        log_src.reshape(s_tile), log_tgt.reshape(t_tile), n_tgt,
    )
    lse = lax.all_to_all(lse, TURNED, 0, 0, tiled=True)
    f, fcol, lse = run_cols(order, scores, lse, log_src, n_src, t_cols)
    lse = lax.all_to_all(lse, "src", 0, 0, tiled=True)
    c, sums = run_map(order, scores, tgt_t, lse, log_tgt, fcol, n_tgt)
    sums = lax.all_to_all(sums, TURNED, 0, 0, tiled=True)
    part, chunk = width // GROUPS, sums.shape[2]
    sums = call(
        functools.partial(merge_kernel, part),
        jax.ShapeDtypeStruct(sums.shape, BF16),
        [pltpu.VMEM((n_tgt, chunk), F32), pltpu.VMEM((CHUNK, chunk), F32)],
        [VMEM],
        sums,
    )
    sums = lax.all_to_all(sums, TURNED, 0, 0, tiled=True)
    mapped, mass = call(
        functools.partial(final_kernel, part),
        (jax.ShapeDtypeStruct((width, s_rows), BF16), jax.ShapeDtypeStruct(s_tile, F32)),
        [pltpu.VMEM((-(-width // 8) * 8, chunk), F32)],
        [VMEM],
        sums,
    )
    return f.reshape(s_rows), c.reshape(t_cols), mapped.T, mass.reshape(s_rows)


def solution(mesh):
    across = min(4, mesh.shape["tgt"])
    parts = mesh.devices.reshape(mesh.shape["tgt"] // across, across, mesh.shape["src"])
    return jax.shard_map(
        local,
        mesh=Mesh(parts, (*TGT, "src")),
        in_specs=(
            P("src", None),
            P(TGT, None),
            P(TGT),
            P("src"),
            P(TGT),
            P("src", None),
            P("src"),
        ),
        out_specs=(P("src"), P(TGT), P("src", None), P("src")),
        check_vma=False,
    )
```

```python
import functools
import itertools

import jax
import jax.numpy as jnp
from jax import lax
from jax.experimental import pallas as pl
from jax.experimental.pallas import tpu as pltpu
from jax.sharding import PartitionSpec as P

BLOCK = 512
LANES = 128
EPS = 0.2
INV = 5.0
LN2 = 0.6931471805599453
SCALE = INV / LN2
STRIP = 32
PART = 512
COUNT = 127
BY_COLUMN = 64
BY_ROW = 96
TINY = 1e-27
NEG = -1e30
GROUPS = 4
CHUNK = 80
NT = (((1,), (1,)), ((), ()))
F32 = jnp.float32
BF16 = jnp.bfloat16


def logsum(values, axis):
    peak = jnp.max(values, axis=axis, keepdims=True)
    return peak + jnp.log(jnp.sum(jnp.exp(values - peak), axis=axis, keepdims=True))


def safe_log(peak, total):
    return jnp.where(total > 0.0, peak * LN2 + jnp.log(jnp.where(total > 0.0, total, 1.0)), NEG)


def lane_parts(tile):
    return [tile[:, k * LANES : (k + 1) * LANES] for k in range(tile.shape[1] // LANES)]


def three_parts(value):
    high = value.astype(BF16).astype(F32)
    rest = value - high
    middle = rest.astype(BF16).astype(F32)
    return high, middle, rest - middle


def pick(order_ref, i, columns):
    place = order_ref[0, jnp.minimum(i, COUNT - 1)]
    return place, place // columns, place % columns, i < order_ref[0, COUNT]


def in_turn(order_ref, columns, make, use):
    tile = functools.partial(pick, order_ref, columns=columns)
    starts = range(0, BLOCK, PART)
    for start in starts:
        make(0, tile(0), start)

    def step(k, carry):
        i = 2 * k
        for start in starts:
            make(1, tile(i + 1), start)
            use(0, tile(i), start)
        for start in starts:
            make(0, tile(i + 2), start)
            use(1, tile(i + 1), start)
        return carry

    count = order_ref[0, COUNT]
    lax.fori_loop(0, count // 2, step, 0)

    @pl.when(count % 2 == 1)
    def _():
        for start in starts:
            use(0, tile(count - 1), start)


def each(order_ref, columns, use):
    tile = functools.partial(pick, order_ref, columns=columns)

    def step(k, carry):
        use(tile(2 * k))
        use(tile(2 * k + 1))
        return carry

    count = order_ref[0, COUNT]
    lax.fori_loop(0, count // 2, step, 0)

    @pl.when(count % 2 == 1)
    def _():
        use(tile(count - 1))


def my_place():
    return lax.axis_index("tgt").astype(jnp.int32)


def block_of(index):
    return pl.ds(pl.multiple_of(index * BLOCK, BLOCK), BLOCK)


def row_kernel(
    count_hbm, ids_hbm, src_hbm, tgt_hbm, g_hbm, log_src_hbm, log_tgt_hbm,
    scores_ref, out_ref, list_ref, log_src_ref, log_tgt_ref,
    order_ref, count_ref, ids_ref, src_ref, tgt_ref, g_ref, pad, rows_ref, peak, total, packed, slot0, slot1, sems,
):
    pairs = (
        (count_hbm, count_ref), (ids_hbm, ids_ref), (src_hbm, src_ref), (tgt_hbm, tgt_ref),
        (g_hbm, g_ref), (log_src_hbm, log_src_ref), (log_tgt_hbm, log_tgt_ref),
    )
    copies = [pltpu.make_async_copy(x, y, sems.at[i]) for i, (x, y) in enumerate(pairs)]
    for copy in copies:
        copy.start()
    width, s_rows = src_ref.shape
    blocks, columns = s_rows // BLOCK, tgt_ref.shape[1] // BLOCK
    peak[...] = jnp.full_like(peak, NEG)
    total[...] = jnp.zeros_like(total)

    copies[0].wait()
    copies[1].wait()
    first = my_place() * columns
    lane = lax.broadcasted_iota(jnp.int32, (1, ids_ref.shape[1]), 1)
    live = []
    for b in range(blocks):
        rel = jnp.where(lane < count_ref[b], ids_ref[b : b + 1, :] - first, -1)
        for t in range(columns):
            live.append(jnp.max(jnp.where(rel == t, 1.0, 0.0)) > 0.0)
    latest = jnp.int32(0)
    for place, there in enumerate(live):
        latest = jnp.where(there, place, latest)
    for i in range(len(live) + 2):
        order_ref[0, i] = latest
    count = jnp.int32(0)
    column = lax.broadcasted_iota(jnp.int32, list_ref.shape, 1)
    listed = jnp.full(list_ref.shape, latest)
    for place, there in enumerate(live):
        value = jnp.where(there, place, latest)
        order_ref[0, count] = value
        listed = jnp.where(column == count, value, listed)
        count = count + there.astype(jnp.int32)
    order_ref[0, COUNT] = count
    listed = jnp.where(column == COUNT, count, listed)
    for t in range(columns):
        there = functools.reduce(jnp.logical_or, live[t::columns])
        listed = jnp.where(column == BY_COLUMN + t, there.astype(jnp.int32), listed)
    for b in range(blocks):
        there = functools.reduce(jnp.logical_or, live[b * columns : (b + 1) * columns])
        listed = jnp.where(column == BY_ROW + b, there.astype(jnp.int32), listed)
    list_ref[...] = listed

    copies[2].wait()
    edge = width // 8 * 8
    pad[edge:, :] = jnp.zeros_like(pad[edge:, :])
    pad[:width, :] = src_ref[...].astype(F32)
    for k in range(s_rows // LANES):
        piece = pad[:, k * LANES : (k + 1) * LANES]
        rows_ref[k * LANES : (k + 1) * LANES, :] = piece.T.astype(BF16)
    for copy in copies[3:]:
        copy.wait()

    slots = (slot0, slot1)

    def make(n, tile, start):
        place, b, t, there = tile
        at = slice(start, start + PART)
        rows = rows_ref[pl.ds(pl.multiple_of(b * BLOCK + start, PART), PART), :]
        values = jnp.dot(rows[:, :width], tgt_ref[:, block_of(t)], preferred_element_type=F32)
        slots[n][at, :] = values
        scores_ref[place, at, :] = values

    def use(n, tile, start):
        place, b, t, there = tile
        g = jnp.where(there, g_ref[:, block_of(t)] * SCALE, 2 * NEG)
        for r in range(start, start + PART, STRIP):
            at = slice(r, r + STRIP)
            z = lane_parts(slots[n][at, :] * SCALE + g)
            old = peak[b, at, :]
            new = functools.reduce(jnp.maximum, z, old)
            peak[b, at, :] = new
            total[b, at, :] = total[b, at, :] * jnp.exp2(old - new) + sum(jnp.exp2(part - new) for part in z)

    in_turn(order_ref, columns, make, use)
    per_block = BLOCK // LANES
    for b in range(blocks):
        turned = peak[b].T
        top = jnp.max(turned, axis=0, keepdims=True)
        mass = jnp.sum(total[b].T * jnp.exp2(turned - top), axis=0, keepdims=True)
        for k, part in enumerate(lane_parts(safe_log(top, mass))):
            packed[b * per_block + k : b * per_block + k + 1, :] = part
    out_ref[...] = jnp.broadcast_to(packed[...][None], out_ref.shape)


def too_small(order_ref, start, masses):
    kept = [jnp.where(order_ref[0, start + i] > 0, mass, 1.0) for i, mass in enumerate(masses)]
    return jnp.min(functools.reduce(jnp.minimum, kept)) < TINY


def col_kernel(
    list_ref, scores_ref, lse_ref, log_ref, f_hbm, fcol, out_ref, order_ref, f_ref, peak, total, packed, slot0, slot1, sems
):
    listed = pltpu.make_async_copy(list_ref, order_ref, sems.at[0])
    listed.start()
    f = EPS * log_ref[...] - EPS * logsum(lse_ref[...], 0)[0]
    f_ref[...] = f
    kept = pltpu.make_async_copy(f_ref, f_hbm, sems.at[1])
    kept.start()
    for k in range(f.shape[0]):
        row = jnp.broadcast_to(f[k : k + 1, :] * SCALE, (LANES, LANES))
        fcol[k * LANES : (k + 1) * LANES, :] = row.T
    total[...] = jnp.zeros_like(total)
    columns = peak.shape[0]
    per_block = BLOCK // LANES

    def logits(tile, r):
        place, b, t, there = tile
        extra = jnp.where(there, 0.0, 2 * NEG)
        own = fcol[pl.ds(pl.multiple_of(b * BLOCK + r, STRIP), STRIP), :] + extra
        return scores_ref[place, r : r + STRIP, :] * SCALE + jnp.concatenate([own] * per_block, axis=1)

    def by_eight(values):
        return values.reshape(STRIP // 8, 8, BLOCK)

    def use(tile):
        sums = [total[tile[2]], jnp.zeros((8, BLOCK), F32)]
        for i, r in enumerate(range(0, BLOCK, STRIP)):
            sums[i % 2] = sums[i % 2] + jnp.sum(by_eight(jnp.exp2(logits(tile, r))), axis=0)
        total[tile[2]] = sums[0] + sums[1]

    listed.wait()
    each(order_ref, columns, use)

    def pack(t, top, mass):
        for k, part in enumerate(lane_parts(safe_log(top, mass))):
            packed[t * per_block + k : t * per_block + k + 1, :] = part

    masses = [jnp.sum(total[t], axis=0, keepdims=True) for t in range(columns)]
    for t in range(columns):
        pack(t, 0.0, masses[t])

    @pl.when(too_small(order_ref, BY_COLUMN, masses))
    def _():
        peak[...] = jnp.full_like(peak, NEG)
        total[...] = jnp.zeros_like(total)

        def scaled(slot, tile):
            t = tile[2]
            old = peak[t]
            tops = [old] * 2
            for i, r in enumerate(range(0, BLOCK, STRIP)):
                y = logits(tile, r)
                slot[r : r + STRIP, :] = y
                tops[i % 2] = jnp.maximum(tops[i % 2], jnp.max(by_eight(y), axis=0))
            new = jnp.maximum(*tops)
            peak[t] = new
            sums = [total[t] * jnp.exp2(old - new), jnp.zeros_like(new)]
            for i, r in enumerate(range(0, BLOCK, STRIP)):
                y = by_eight(slot[r : r + STRIP, :])
                sums[i % 2] = sums[i % 2] + jnp.sum(jnp.exp2(y - new[None]), axis=0)
            total[t] = sums[0] + sums[1]

        slots = itertools.cycle((slot0, slot1))
        each(order_ref, columns, lambda tile: scaled(next(slots), tile))
        for t in range(columns):
            top = jnp.max(peak[t], axis=0, keepdims=True)
            pack(t, top, jnp.sum(total[t] * jnp.exp2(peak[t] - top), axis=0, keepdims=True))

    out_ref[...] = jnp.broadcast_to(packed[...][None], out_ref.shape)
    kept.wait()


def map_kernel(
    list_ref, scores_ref, tgt_ref, lse_ref, log_ref, fcol, c_hbm, out_ref,
    order_ref, c_ref, crow, peak, shift, tops, mass_ref, denom, numer, buf, part0, part1, sems,
):
    width = tgt_ref.shape[0]
    listed = pltpu.make_async_copy(list_ref, order_ref, sems.at[0])
    listed.start()
    c = EPS * log_ref[...] - EPS * logsum(lse_ref[...], 0)[0]
    c_ref[...] = c
    kept = pltpu.make_async_copy(c_ref, c_hbm, sems.at[1])
    kept.start()
    for k in range(c.shape[0]):
        crow[:, k * LANES : (k + 1) * LANES] = c[k : k + 1, :] * SCALE
    blocks, columns = peak.shape[0], tgt_ref.shape[1] // BLOCK
    slots = (part0, part1)

    def strip(b, r):
        return pl.ds(pl.multiple_of(b * BLOCK + r, STRIP), STRIP)

    def weigh(shift_ref, n, tile, start):
        place, b, t, there = tile
        extra = jnp.where(there, 0.0, 2 * NEG)
        own = crow[:, block_of(t)]
        for r in range(start, start + PART, STRIP):
            at = slice(r, r + STRIP)
            moved = shift_ref[strip(b, r), :] + extra
            values = scores_ref[place, at, :] * SCALE + own
            weights = [jnp.exp2(part + moved).astype(BF16) for part in lane_parts(values)]
            slots[n][at, :] = jnp.concatenate(weights, axis=1)
            denom[b, at, :] = denom[b, at, :] + sum(part.astype(F32) for part in weights)

    def add(n, tile, start):
        place, b, t, there = tile
        at = slice(start, start + PART)
        numer[b, :, at] = numer[b, :, at] + lax.dot_general(
            tgt_ref[:, block_of(t)], slots[n][at, :], NT, preferred_element_type=F32
        )

    def totals(shift_ref):
        denom[...] = jnp.zeros_like(denom)
        numer[...] = jnp.zeros_like(numer)

        @pl.when(order_ref[0, COUNT] > 0)
        def _():
            in_turn(order_ref, columns, functools.partial(weigh, shift_ref), add)

        for b in range(blocks):
            mass_ref[b : b + 1, :] = jnp.sum(denom[b].T, axis=0, keepdims=True)

    def masses():
        return [mass_ref[b : b + 1, :] for b in range(blocks)]

    tops[...] = jnp.zeros_like(tops)
    listed.wait()
    totals(fcol)

    @pl.when(too_small(order_ref, BY_ROW, masses()))
    def _():
        peak[...] = jnp.full_like(peak, NEG)

        def first(tile):
            place, b, t, there = tile
            own = crow[:, block_of(t)]
            for r in range(0, BLOCK, STRIP):
                at = slice(r, r + STRIP)
                parts = [part + fcol[strip(b, r), :] for part in lane_parts(scores_ref[place, at, :] * SCALE + own)]
                peak[b, at, :] = functools.reduce(jnp.maximum, parts, peak[b, at, :])

        each(order_ref, columns, first)
        for b in range(blocks):
            rows = slice(b * BLOCK, (b + 1) * BLOCK)
            tops[b : b + 1, :] = jnp.max(peak[b].T, axis=0, keepdims=True)
            shift[rows, :] = fcol[rows, :] - jnp.max(peak[b], axis=1, keepdims=True)
        totals(shift)

    part = width // GROUPS
    chunk = out_ref.shape[2]
    for b, mass in enumerate(masses()):
        inverse = 1.0 / jnp.where(mass > 0.0, mass, 1.0)
        logs = three_parts(safe_log(tops[b : b + 1, :], mass))
        for k in range(GROUPS):
            buf[:part, :] = numer[b, k * part : (k + 1) * part, :] * inverse
            for j in range(3):
                buf[part + j : part + j + 1, :] = logs[j]
            buf[part + 3 :, :] = jnp.zeros_like(buf[part + 3 :, :])
            for r in range(BLOCK // chunk):
                place = (b * (BLOCK // chunk) + r) * GROUPS + k
                out_ref[place] = buf[:, r * chunk : (r + 1) * chunk].astype(BF16)
    kept.wait()


def merge_kernel(part, in_ref, out_ref, logs, buf):
    count = in_ref.shape[0]
    for t in range(count):
        tail = in_ref[t].astype(F32)
        logs[t : t + 1, :] = tail[part : part + 1] + tail[part + 1 : part + 2] + tail[part + 2 : part + 3]
    top = jnp.max(logs[...], axis=0, keepdims=True)
    share = jnp.exp(logs[...] - top)
    mass = jnp.sum(share, axis=0, keepdims=True)
    logs[...] = share / mass
    acc = jnp.zeros(in_ref.shape[1:], F32)
    for t in range(count):
        acc = acc + in_ref[t].astype(F32) * logs[t : t + 1, :]
    buf[...] = acc
    for j, piece in enumerate(three_parts(top + jnp.log(mass))):
        buf[part + j : part + j + 1, :] = piece
    out_ref[...] = jnp.broadcast_to(buf[...].astype(BF16)[None], out_ref.shape)


def final_kernel(part, in_ref, mapped_ref, mass_ref, buf):
    chunk = in_ref.shape[2]
    per = chunk // LANES
    for r in range(in_ref.shape[0] // GROUPS):
        for k in range(GROUPS):
            piece = in_ref[r * GROUPS + k].astype(F32)
            buf[k * part : (k + 1) * part, :] = piece[:part]
        mapped_ref[:, r * chunk : (r + 1) * chunk] = buf[: GROUPS * part, :].astype(BF16)
        total = piece[part : part + 1] + piece[part + 1 : part + 2] + piece[part + 2 : part + 3]
        for j in range(per):
            mass_ref[r * per + j : r * per + j + 1, :] = total[:, j * LANES : (j + 1) * LANES]


VMEM = pl.BlockSpec(memory_space=pltpu.VMEM)
HBM = pl.BlockSpec(memory_space=pltpu.HBM)
PARAMS = pltpu.CompilerParams(vmem_limit_bytes=24 * 1024 * 1024)


def call(kernel, out_shape, scratch, specs, *args, outs=None):
    return pl.pallas_call(
        kernel,
        out_shape=out_shape,
        in_specs=specs,
        out_specs=jax.tree.map(lambda _: VMEM, out_shape) if outs is None else outs,
        scratch_shapes=scratch,
        compiler_params=PARAMS,
    )(*args)


def run_rows(count, ids, src_t, tgt_t, g, log_src, log_tgt, n_tgt):
    (width, s_rows), t_cols = src_t.shape, tgt_t.shape[1]
    blocks, columns = s_rows // BLOCK, t_cols // BLOCK
    padded = -(-width // LANES) * LANES
    s_tile = (s_rows // LANES, LANES)
    return call(
        row_kernel,
        (
            jax.ShapeDtypeStruct((blocks * columns, BLOCK, BLOCK), F32),
            jax.ShapeDtypeStruct((n_tgt, *s_tile), F32),
            jax.ShapeDtypeStruct((1, LANES), jnp.int32),
            jax.ShapeDtypeStruct(log_src.shape, F32),
            jax.ShapeDtypeStruct(log_tgt.shape, F32),
        ),
        [
            pltpu.SMEM((1, LANES), jnp.int32),
            pltpu.SMEM(count.shape, jnp.int32),
            pltpu.VMEM(ids.shape, jnp.int32),
            pltpu.VMEM(src_t.shape, BF16),
            pltpu.VMEM(tgt_t.shape, BF16),
            pltpu.VMEM(g.shape, F32),
            pltpu.VMEM((padded, s_rows), F32),
            pltpu.VMEM((s_rows, padded), BF16),
            pltpu.VMEM((blocks, BLOCK, LANES), F32),
            pltpu.VMEM((blocks, BLOCK, LANES), F32),
            pltpu.VMEM(s_tile, F32),
            pltpu.VMEM((BLOCK, BLOCK), F32),
            pltpu.VMEM((BLOCK, BLOCK), F32),
            pltpu.SemaphoreType.DMA((7,)),
        ],
        [HBM] * 7,
        *(pltpu.with_memory_space_constraint(x, pltpu.HBM) for x in (count, ids, src_t, tgt_t, g, log_src, log_tgt)),
    )


def run_cols(order, scores, lse, log_src, n_src, t_cols):
    s_tile, s_rows = log_src.shape, log_src.size
    t_tile, columns = (t_cols // LANES, LANES), t_cols // BLOCK
    return call(
        col_kernel,
        (
            jax.ShapeDtypeStruct(s_tile, F32),
            jax.ShapeDtypeStruct((s_rows, LANES), F32),
            jax.ShapeDtypeStruct((n_src, *t_tile), F32),
        ),
        [
            pltpu.SMEM((1, LANES), jnp.int32),
            pltpu.VMEM(s_tile, F32),
            pltpu.VMEM((columns, 8, BLOCK), F32),
            pltpu.VMEM((columns, 8, BLOCK), F32),
            pltpu.VMEM(t_tile, F32),
            pltpu.VMEM((BLOCK, BLOCK), F32),
            pltpu.VMEM((BLOCK, BLOCK), F32),
            pltpu.SemaphoreType.DMA((2,)),
        ],
        [VMEM, VMEM, VMEM, VMEM],
        order, scores, lse, log_src,
        outs=(HBM, VMEM, VMEM),
    )


def run_map(order, scores, tgt_t, lse, log_tgt, fcol, n_tgt):
    s_rows = fcol.shape[0]
    t_tile, (width, t_cols) = log_tgt.shape, tgt_t.shape
    blocks, columns = s_rows // BLOCK, t_cols // BLOCK
    chunk = s_rows * GROUPS // n_tgt
    return call(
        map_kernel,
        (jax.ShapeDtypeStruct(t_tile, F32), jax.ShapeDtypeStruct((n_tgt, CHUNK, chunk), BF16)),
        [
            pltpu.SMEM((1, LANES), jnp.int32),
            pltpu.VMEM(t_tile, F32),
            pltpu.VMEM((1, t_cols), F32),
            pltpu.VMEM((blocks, BLOCK, LANES), F32),
            pltpu.VMEM(fcol.shape, F32),
            pltpu.VMEM((blocks, BLOCK), F32),
            pltpu.VMEM((blocks, BLOCK), F32),
            pltpu.VMEM((blocks, BLOCK, LANES), F32),
            pltpu.VMEM((blocks, width, BLOCK), F32),
            pltpu.VMEM((CHUNK, BLOCK), F32),
            pltpu.VMEM((BLOCK, BLOCK), BF16),
            pltpu.VMEM((BLOCK, BLOCK), BF16),
            pltpu.SemaphoreType.DMA((2,)),
        ],
        [VMEM] * 6,
        order, scores, tgt_t, lse, log_tgt, fcol,
        outs=(HBM, VMEM),
    )


def local(src_emb, tgt_emb, g_init, log_src, log_tgt, cand_ids, cand_count):
    s_rows, width = src_emb.shape
    t_cols = tgt_emb.shape[0]
    n_tgt, n_src = lax.axis_size("tgt"), lax.axis_size("src")
    src_t, tgt_t = src_emb.T, tgt_emb.T
    s_tile = (s_rows // LANES, LANES)
    t_tile = (t_cols // LANES, LANES)

    scores, lse, order, log_src, log_tgt = run_rows(
        cand_count, cand_ids, src_t, tgt_t, g_init.reshape(1, t_cols),
        log_src.reshape(s_tile), log_tgt.reshape(t_tile), n_tgt,
    )
    lse = lax.all_to_all(lse, "tgt", 0, 0, tiled=True)
    f, fcol, lse = run_cols(order, scores, lse, log_src, n_src, t_cols)
    lse = lax.all_to_all(lse, "src", 0, 0, tiled=True)
    c, sums = run_map(order, scores, tgt_t, lse, log_tgt, fcol, n_tgt)
    sums = lax.all_to_all(sums, "tgt", 0, 0, tiled=True)
    part, chunk = width // GROUPS, sums.shape[2]
    sums = call(
        functools.partial(merge_kernel, part),
        jax.ShapeDtypeStruct(sums.shape, BF16),
        [pltpu.VMEM((n_tgt, chunk), F32), pltpu.VMEM((CHUNK, chunk), F32)],
        [VMEM],
        sums,
    )
    sums = lax.all_to_all(sums, "tgt", 0, 0, tiled=True)
    mapped, mass = call(
        functools.partial(final_kernel, part),
        (jax.ShapeDtypeStruct((width, s_rows), BF16), jax.ShapeDtypeStruct(s_tile, F32)),
        [pltpu.VMEM((-(-width // 8) * 8, chunk), F32)],
        [VMEM],
        sums,
    )
    return f.reshape(s_rows), c.reshape(t_cols), mapped.T, mass.reshape(s_rows)


def solution(mesh):
    return jax.shard_map(
        local,
        mesh=mesh,
        in_specs=(
            P("src", None),
            P("tgt", None),
            P("tgt"),
            P("src"),
            P("tgt"),
            P("src", None),
            P("src"),
        ),
        out_specs=(P("src"), P("tgt"), P("src", None), P("src")),
        check_vma=False,
    )
```
